32 devices in a mesh: sec: 4 (over y, x), dev: 8 (over z, core).
Axes of the slice: x: 2, y: 2, z: 4, core: 2. Of those that a mesh axis runs over, the one named last changes fastest.
Arguments:
- tile_inverse: bfloat16 [32, 4, 512, 512], P(('sec', 'dev'))
- link_coupling: bfloat16 [32, 512, 2048], P(('sec', 'dev')), may hold values from -0.125 to 0.125
- link_panels: int32 [32, 4], P(('sec', 'dev')), may hold values from 0 to 63, all different within a row
- leaf_rhs: bfloat16 [32, 48, 2048], P(('sec', 'dev')), may hold values from -6 to 6
- leaf_scale: float32 [32, 2048], P(('sec', 'dev')), may hold values from 0.1 to 0.5
- link_scale: float32 [8192], replicated, may hold values from 0.2 to 2
- link_inverse: bfloat16 [8192, 8192], P('sec', 'dev'), as said below
Outputs:
- leaf_step: bfloat16 [32, 48, 2048], P(('sec', 'dev'))
- link_step: bfloat16 [48, 8192], P(None, 'dev')
The draws below stay inside these ranges and needn't reach their ends.
Inputs may be any that keep to these rules, and one draw needn't show every extreme that they name: `link_panels`: the 4 panels of one block are different. link_inverse is symmetric.
All inputs are finite; a program needn't handle non-finite values.
Results may differ from the reference program's by a relative error of at most 0.02.
Values may be sent and summed in bfloat16 or wider, within the bound.
A program may use at most 64 MiB of HBM per device.

```python
import math
import jax
import jax.numpy as jnp
from jax import lax

NB = 2048
TILE = 512
LINK = 8192
PANEL = 128
PB = 4
COLS = 48
SOLVES = 5
BLOCKS = 32


def draw_tile_inverse(key, part):
    first_key, second_key = jax.random.split(jax.random.fold_in(key, 11))
    shape = (BLOCKS, NB // TILE, TILE, TILE)
    noise = jax.random.truncated_normal(first_key, -4.0, 4.0, shape, jnp.float32)
    diag_values = jnp.exp(jax.random.uniform(second_key, (BLOCKS, NB // TILE, TILE), jnp.float32, math.log(0.5), math.log(2.0)))
    tiles = noise * (0.5 / math.sqrt(TILE)) + diag_values[..., None] * jnp.eye(TILE, dtype=jnp.float32)
    return tiles.astype(jnp.bfloat16)


def draw_link_inverse(key, part):
    first_key, second_key = jax.random.split(jax.random.fold_in(key, 23))
    noise = jax.random.normal(first_key, (LINK, LINK), jnp.float32)
    diag_values = jnp.exp(jax.random.uniform(second_key, (LINK,), jnp.float32, math.log(0.1), math.log(0.3)))
    symmetric = (noise + noise.T) * (0.05 / math.sqrt(2.0 * LINK))
    return (symmetric + jnp.diag(diag_values)).astype(jnp.bfloat16)


def steps_of(stream_key, extent, pieces, low, top_value):
    def one(position, blocks):
        steps = jax.random.uniform(jax.random.fold_in(jax.random.fold_in(stream_key, 6), position), (blocks,), jnp.float32, low / len(pieces), top_value / len(pieces))
        return jnp.repeat(jnp.exp(steps), extent[position] // blocks).reshape((-1,) + (1,) * (len(extent) - position - 1))

    gain = one(*pieces[0])
    for cut in pieces[1:]:
        gain = gain * one(*cut)
    return gain


def different_ones(stream_key, rows, number_of, top, lift):
    order = jax.random.permutation(jax.random.fold_in(stream_key, 1), number_of)
    pull = order
    for power in range(3):
        pull = pull * pull // number_of
    pull = pull * lift // number_of
    chance = jax.random.randint(jax.random.fold_in(stream_key, 2), (rows, number_of), 0, 4096) + pull
    sure = jax.random.permutation(jax.random.fold_in(stream_key, 3), rows)[jnp.arange(number_of) % rows]
    chance = jnp.where(jnp.arange(rows)[:, None] == sure[None, :], 1 << 14, chance)
    score = chance * number_of + jnp.arange(number_of)
    return lax.top_k(score.astype(jnp.int32), top)[1].astype(jnp.int32)


def gaussian(key, shape, scale, limit, shards=(), held_as=jnp.bfloat16):
    gain = steps_of(key, shape, shards, -0.22, 0.18) if shards else 1.0
    values = jax.random.normal(key, shape, jnp.float32) * scale * gain
    return jnp.minimum(jnp.maximum(values, -limit), limit).astype(held_as)


def setup_inputs(seed: int = 0) -> dict:
    keys = jax.random.split(jax.random.key(seed), 8)
    return {
        "tile_inverse": draw_tile_inverse(jax.random.fold_in(keys[7], 71), 0),
        "link_coupling": gaussian(keys[1], (BLOCKS, PB * PANEL, NB), NB ** -0.5, 0.125, ((0, 32),)),
        "link_panels": different_ones(keys[2], BLOCKS, LINK // PANEL, PB, 0),
        "leaf_rhs": gaussian(keys[3], (BLOCKS, COLS, NB), 1.0, 6.0, ((0, 32),)),
        "leaf_scale": jnp.clip(jnp.exp(math.log(0.5) - 1.609438 * jax.random.uniform(keys[4], (BLOCKS, NB), jnp.float32) ** steps_of(keys[4], (BLOCKS, NB), ((0, 32),), -0.2, 0.2)), 0.1, 0.5),
        "link_scale": jnp.clip(jnp.exp(jax.random.uniform(keys[5], (LINK,), jnp.float32, math.log(0.2), math.log(2.0))), 0.2, 2.0),
        "link_inverse": draw_link_inverse(jax.random.fold_in(keys[7], 71), 0),
    }


def apply_tiles(tile_inv, vectors):
    columns = vectors.shape[0]
    blocked = vectors.astype(jnp.float32).reshape(columns, NB // TILE, TILE)
    result = jnp.einsum("tab,ctb->cta", tile_inv.astype(jnp.float32), blocked)
    return result.reshape(columns, NB)


def reference(tile_inverse, link_coupling, link_panels, leaf_rhs, leaf_scale, link_scale, link_inverse):
    panel_count = LINK // PANEL
    selectors = (link_panels[:, :, None] == jnp.arange(panel_count, dtype=jnp.int32)[None, None, :]).astype(jnp.float32)
    previous = jnp.zeros(leaf_rhs.shape, jnp.bfloat16)
    linking = jnp.zeros((COLS, LINK), jnp.bfloat16)
    for solve_index in range(SOLVES):
        corrected = (leaf_rhs.astype(jnp.float32) - leaf_scale[:, None, :] * previous.astype(jnp.float32)).astype(jnp.bfloat16)

        def forward(summed, block_items):
            tile_inv, coupling, selector, right_side = block_items
            solved = apply_tiles(tile_inv, right_side).astype(jnp.bfloat16)
            touched = jnp.dot(solved, coupling.T, preferred_element_type=jnp.float32)
            spread = jnp.einsum("csr,sq->cqr", touched.reshape(COLS, PB, PANEL), selector)
            spread = spread.reshape(COLS, LINK).astype(jnp.bfloat16)
            return summed + spread.astype(jnp.float32), None

        summed, ignored = lax.scan(forward, jnp.zeros((COLS, LINK), jnp.float32),
                                   (tile_inverse, link_coupling, selectors, corrected))
        link_side = -link_scale[None, :] * linking.astype(jnp.float32)
        link_rhs = (link_side - summed).astype(jnp.bfloat16)
        linking = jnp.dot(link_rhs, link_inverse, preferred_element_type=jnp.float32).astype(jnp.bfloat16)
        link_now = linking

        def backward(block_items):
            tile_inv, coupling, selector, right_side = block_items
            picked = jnp.einsum("cqr,sq->csr", link_now.astype(jnp.float32).reshape(COLS, panel_count, PANEL), selector)
            picked = picked.reshape(COLS, PB * PANEL).astype(jnp.bfloat16)
            pushed = jnp.dot(picked, coupling, preferred_element_type=jnp.float32)
            reduced = (right_side.astype(jnp.float32) - pushed).astype(jnp.bfloat16)
            return apply_tiles(tile_inv, reduced).astype(jnp.bfloat16)

        previous = lax.map(backward, (tile_inverse, link_coupling, selectors, corrected))
    return previous, linking
```

```python
import functools

import jax
import jax.numpy as jnp
from jax import lax
from jax.experimental import pallas as pl
from jax.experimental.pallas import tpu as pltpu
from jax.sharding import PartitionSpec as P

SOLVES = 5
F32 = jnp.float32
BF16 = jnp.bfloat16


def nn(a, b):
    return lax.dot_general(a, b, (((1,), (0,)), ((), ())), preferred_element_type=F32)


def nt(a, b):
    return lax.dot_general(a, b, (((1,), (1,)), ((), ())), preferred_element_type=F32)


def kernel(
    n_sec, n_dev, per,
    panels_ref, slot_ref, tile_ref, coup_ref, rhs_ref, scale_ref, lscale_ref, linv_hbm,
    leaf_out, link_out,
    linv, slot_v, slot_s, tbuf, rsend, rrecv, hbuf, lsend, lrecv, link,
    mmat, qmat, kmat, kacc, base, solved, umat, picked, part,
    in_sem, slot_sem, slot_send, slot_recv,
    t_send, t_recv, r_send, r_recv, h_send, h_recv, l_send, l_recv,
    z_send, z_recv, g_send, g_recv, c_send, c_recv,
):
    s = lax.axis_index("sec")
    d = lax.axis_index("dev")
    n_z = n_dev // 2
    z = d // 2
    c = d % 2
    partner = z * 2 + (1 - c)
    pb = tbuf.shape[2] - 1
    tiles, tile = tile_ref.shape[0], tile_ref.shape[1]
    panel = tbuf.shape[4]
    per_sec = n_dev * per
    per_dev = n_sec * per

    def remote(src, dst, send, recv, target):
        return pltpu.make_async_remote_copy(
            src_ref=src, dst_ref=dst, send_sem=send, recv_sem=recv,
            device_id=target, device_id_type=pl.DeviceIdType.MESH,
        )

    linv_copy = pltpu.make_async_copy(linv_hbm, linv, in_sem)
    linv_copy.start()

    barrier = pltpu.get_barrier_semaphore()
    for j in range(1, n_dev):
        pl.semaphore_signal(barrier, inc=1, device_id={"dev": (d + j) % n_dev},
                            device_id_type=pl.DeviceIdType.MESH)
    for j in range(1, n_sec):
        pl.semaphore_signal(barrier, inc=1, device_id={"sec": (s + j) % n_sec},
                            device_id_type=pl.DeviceIdType.MESH)

    zero_panel = jnp.zeros(tbuf.shape[3:], BF16)
    for k in range(SOLVES):
        for i in range(n_dev):
            tbuf[k, i, pb] = zero_panel
    own_rhs = s * per_sec + d * per
    for j in range(per):
        link[0, own_rhs + j] = zero_panel
    slot_v[d] = slot_ref[...]
    first = None
    for t in range(tiles):
        cols = pl.ds(t * tile, tile)
        value = nt(rhs_ref[:, cols], tile_ref[t])
        solved[:, cols] = value
        term = nt(value.astype(BF16), coup_ref[:, cols])
        first = term if first is None else first + term
    base[...] = first
    for q in range(pb):
        tbuf[0, d, q] = first[:, q * panel:(q + 1) * panel].astype(BF16)

    pl.semaphore_wait(barrier, n_dev - 1 + n_sec - 1)

    slot_copies = []
    for j in range(1, n_dev):
        copy = remote(slot_v.at[d], slot_v.at[d], slot_send.at[j], slot_recv.at[j],
                      {"dev": (d + j) % n_dev})
        copy.start()
        slot_copies.append(copy)

    def solve(k, carry):
        sends = []

        t_copies = []
        for j in range(1, n_dev):
            mine = tbuf.at[k, d, pl.ds(0, pb)]
            copy = remote(mine, mine, t_send.at[j], t_recv.at[j], {"dev": (d + j) % n_dev})
            copy.start()
            t_copies.append(copy)
        sends += t_copies

        @pl.when(k == 0)
        def _():
            for t in range(tiles):
                cols = pl.ds(t * tile, tile)
                mmat[:, cols] = nn(coup_ref[:, cols], tile_ref[t]).astype(BF16)
                qmat[:, cols] = nt(coup_ref[:, cols], tile_ref[t]).astype(BF16)
            for copy in slot_copies:
                copy.wait()
            to_smem = pltpu.make_async_copy(slot_v, slot_s, slot_sem)
            to_smem.start()
            to_smem.wait()

        @pl.when(k > 0)
        def _():
            for t in range(tiles):
                cols = pl.ds(t * tile, tile)
                leaf = solved[:, cols] - nn(picked[...], qmat[:, cols])
                x = rhs_ref[:, cols].astype(F32) - scale_ref[:, cols] * leaf
                solved[:, cols] = nt(x.astype(BF16), tile_ref[t])

        for copy in t_copies:
            copy.wait_recv()
        for a in range(n_sec):
            for j in range(per):
                q = a * per_sec + d * per + j
                total = tbuf[k, 0, slot_s[0, 0, q]].astype(F32)
                for i in range(1, n_dev):
                    total = total + tbuf[k, i, slot_s[i, 0, q]].astype(F32)
                rsend[k, a, j] = total.astype(BF16)

        r_copies = []
        for j in range(1, n_sec):
            to = (s + j) % n_sec
            copy = remote(rsend.at[k, to], rrecv.at[k, s], r_send.at[j], r_recv.at[j], {"sec": to})
            copy.start()
            r_copies.append(copy)
        sends += r_copies
        rhs_part = []
        for j in range(per):
            prev = link[k, own_rhs + j].astype(F32)
            rhs_part.append(-lscale_ref[own_rhs + j] * prev - rsend[k, s, j].astype(F32))
        for copy in r_copies:
            copy.wait_recv()
        for j in range(per):
            total = rhs_part[j]
            for i in range(1, n_sec):
                total = total - rrecv[k, (s + i) % n_sec, j].astype(F32)
            hbuf[k, d, j] = total.astype(BF16)

        h_copies = []
        for j in range(1, n_dev):
            mine = hbuf.at[k, d]
            copy = remote(mine, mine, h_send.at[j], h_recv.at[j], {"dev": (d + j) % n_dev})
            copy.start()
            h_copies.append(copy)
        sends += h_copies

        @pl.when(k == 0)
        def _():
            linv_copy.wait()

        def multiply(owner):
            left = jnp.concatenate([hbuf[k, owner, j] for j in range(per)], axis=1)
            depth = per * panel
            rows = pl.ds(pl.multiple_of(owner * depth, depth), depth)
            return nn(left, linv[rows, :])

        part[...] = multiply(d)

        @pl.when(k < SOLVES - 1)
        def _():
            total = base[...]
            for t in range(tiles):
                cols = pl.ds(t * tile, tile)
                scaled = (scale_ref[:, cols] * solved[:, cols]).astype(BF16)
                total = total - nt(scaled, mmat[:, cols])
            umat[...] = total

        for j in range(1, n_dev):
            h_copies[j - 1].wait_recv()
            part[...] += multiply((d - j + n_dev) % n_dev)
        for q in range(per_dev):
            lsend[k, q] = part[:, q * panel:(q + 1) * panel].astype(BF16)

        l_copies = []
        for j in range(1, n_sec):
            to = (s + j) % n_sec
            copy = remote(lsend.at[k, pl.ds(to * per, per)], lrecv.at[k, s],
                          l_send.at[j], l_recv.at[j], {"sec": to})
            copy.start()
            l_copies.append(copy)
        sends += l_copies

        @pl.when(k == 0)
        def _():
            for t in range(tiles):
                cols = pl.ds(t * tile, tile)
                scaled = (scale_ref[:, cols] * qmat[:, cols].astype(F32)).astype(BF16)
                term = nt(scaled, mmat[:, cols])
                if t == 0:
                    kacc[...] = term
                else:
                    kacc[...] += term
            kmat[...] = kacc[...].astype(BF16)

        for copy in l_copies:
            copy.wait_recv()
        for j in range(per):
            total = part[:, pl.ds(pl.multiple_of((s * per + j) * panel, panel), panel)]
            for i in range(1, n_sec):
                total = total + lrecv[k, (s + i) % n_sec, j].astype(F32)
            link[k + 1, d * per_dev + s * per + j] = total.astype(BF16)

        def piece(owner, section):
            return link.at[k + 1, pl.ds(owner * per_dev + section * per, per)]

        z_copies = []
        for j in range(1, n_z):
            copy = remote(piece(d, s), piece(d, s), z_send.at[j], z_recv.at[j],
                          {"dev": ((z + j) % n_z) * 2 + c})
            copy.start()
            z_copies.append(copy)
        sends += z_copies
        g_copies = []
        for i in range(n_z):
            owner = ((z - i + n_z) % n_z) * 2 + c
            if i > 0:
                z_copies[i - 1].wait_recv()
            group = []
            for j in range(1, n_sec):
                copy = remote(piece(owner, s), piece(owner, s), g_send.at[i, j], g_recv.at[i, j],
                              {"sec": (s + j) % n_sec})
                copy.start()
                group.append(copy)
            g_copies.append(group)
            sends += group
        c_copies = []
        for i in range(n_z):
            owner = ((z - i + n_z) % n_z) * 2 + c
            for copy in g_copies[i]:
                copy.wait_recv()
            whole = link.at[k + 1, pl.ds(owner * per_dev, per_dev)]
            copy = remote(whole, whole, c_send.at[i], c_recv.at[i], {"dev": partner})
            copy.start()
            c_copies.append(copy)
        sends += c_copies
        for copy in c_copies:
            copy.wait_recv()

        for q in range(pb):
            picked[:, q * panel:(q + 1) * panel] = link[k + 1, panels_ref[0, q]]

        @pl.when(k < SOLVES - 1)
        def _():
            touched = umat[...] + nn(picked[...], kmat[...])
            for q in range(pb):
                tbuf[k + 1, d, q] = touched[:, q * panel:(q + 1) * panel].astype(BF16)

        for copy in sends:
            copy.wait_send()
        return carry

    lax.fori_loop(0, SOLVES, solve, 0)

    for t in range(tiles):
        cols = pl.ds(t * tile, tile)
        leaf_out[:, cols] = (solved[:, cols] - nn(picked[...], qmat[:, cols])).astype(BF16)
    for q in range(per_dev):
        link_out[:, q * panel:(q + 1) * panel] = link[SOLVES, d * per_dev + q]


def fused(n_sec, n_dev, per, tile_inverse, link_coupling, link_panels, leaf_rhs, leaf_scale,
          link_scale, link_inverse):
    pb = link_panels.shape[1]
    rows, nb = link_coupling.shape[1:]
    panel = rows // pb
    cols = leaf_rhs.shape[1]
    total_panels = link_scale.shape[0] // panel
    order = jnp.arange(128, dtype=jnp.int32)
    matches = link_panels[0][:, None] == order[None, :]
    slots = pb - jnp.sum(
        jnp.where(matches, pb - jnp.arange(pb, dtype=jnp.int32)[:, None], 0), axis=0,
        dtype=jnp.int32,
    )
    slots = jnp.broadcast_to(slots[None, :], (8, 128))
    per_dev = n_sec * per
    n_z = n_dev // 2
    vmem = pl.BlockSpec(memory_space=pltpu.VMEM)
    dma = pltpu.SemaphoreType.DMA
    leaf, link = pl.pallas_call(
        functools.partial(kernel, n_sec, n_dev, per),
        out_shape=(
            jax.ShapeDtypeStruct((cols, nb), BF16),
            jax.ShapeDtypeStruct((cols, per_dev * panel), BF16),
        ),
        in_specs=[pl.BlockSpec(memory_space=pltpu.SMEM)] + [vmem] * 6
        + [pl.BlockSpec(memory_space=pl.ANY)],
        out_specs=(vmem, vmem),
        scratch_shapes=[
            pltpu.VMEM(link_inverse.shape, BF16),
            pltpu.VMEM((n_dev, 8, 128), jnp.int32),
            pltpu.SMEM((n_dev, 8, 128), jnp.int32),
            pltpu.VMEM((SOLVES, n_dev, pb + 1, cols, panel), BF16),
            pltpu.VMEM((SOLVES, n_sec, per, cols, panel), BF16),
            pltpu.VMEM((SOLVES, n_sec, per, cols, panel), BF16),
            pltpu.VMEM((SOLVES, n_dev, per, cols, panel), BF16),
            pltpu.VMEM((SOLVES, per_dev, cols, panel), BF16),
            pltpu.VMEM((SOLVES, n_sec, per, cols, panel), BF16),
            pltpu.VMEM((SOLVES + 1, total_panels, cols, panel), BF16),
            pltpu.VMEM((rows, nb), BF16),
            pltpu.VMEM((rows, nb), BF16),
            pltpu.VMEM((rows, rows), BF16),
            pltpu.VMEM((rows, rows), F32),
            pltpu.VMEM((cols, rows), F32),
            pltpu.VMEM((cols, nb), F32),
            pltpu.VMEM((cols, rows), F32),
            pltpu.VMEM((cols, rows), BF16),
            pltpu.VMEM((cols, per_dev * panel), F32),
            dma, dma, dma((n_dev,)), dma((n_dev,)),
            dma((n_dev,)), dma((n_dev,)), dma((n_sec,)), dma((n_sec,)),
            dma((n_dev,)), dma((n_dev,)), dma((n_sec,)), dma((n_sec,)),
            dma((n_z,)), dma((n_z,)), dma((n_z, n_sec)), dma((n_z, n_sec)),
            dma((n_z,)), dma((n_z,)),
        ],
        compiler_params=pltpu.CompilerParams(
            collective_id=0, has_side_effects=True, vmem_limit_bytes=48 * 1024 * 1024
        ),
    )(
        link_panels, slots, tile_inverse[0], link_coupling[0], leaf_rhs[0], leaf_scale,
        link_scale.reshape(total_panels, 1, panel), link_inverse,
    )
    return leaf[None], link


def apply_tiles(tile_inv, vectors):
    columns = vectors.shape[0]
    blocked = vectors.reshape(columns, tile_inv.shape[0], tile_inv.shape[1])
    result = jnp.einsum("tab,ctb->cta", tile_inv, blocked, preferred_element_type=F32)
    return result.reshape(columns, -1)


def plain(tile_inverse, link_coupling, link_panels, leaf_rhs, leaf_scale, link_scale, link_inverse):
    tile_inv, coupling, leaf_gain = tile_inverse[0], link_coupling[0], leaf_scale[0]
    own_panels = link_panels[0]
    pb = own_panels.shape[0]
    panel = coupling.shape[0] // pb
    link_size = link_scale.shape[0]
    panel_count = link_size // panel
    matches = own_panels[:, None] == jnp.arange(panel_count, dtype=jnp.int32)[None, :]
    selector = matches.astype(BF16)
    spreader = matches.astype(F32)
    columns = leaf_rhs.shape[1]
    previous = jnp.zeros(leaf_rhs.shape[1:], BF16)
    linking = jnp.zeros((columns, link_size), BF16)
    for solve_index in range(SOLVES):
        corrected = leaf_rhs[0].astype(F32) - leaf_gain[None, :] * previous.astype(F32)
        corrected = corrected.astype(BF16)
        link_side = -link_scale[None, :] * linking.astype(F32)
        solved = apply_tiles(tile_inv, corrected).astype(BF16)
        touched = jnp.einsum("cn,rn->cr", solved, coupling, preferred_element_type=F32)
        touched = touched.reshape(columns, pb, panel)
        spread = jnp.einsum("csr,sq->cqr", touched, spreader).reshape(columns, link_size)
        section = lax.psum_scatter(
            spread.astype(BF16), "sec", scatter_dimension=1, tiled=True
        ).astype(F32)
        summed = lax.psum(section, "dev")
        width = summed.shape[1]
        own_slab = lax.dynamic_slice_in_dim(link_side, lax.axis_index("sec") * width, width, 1)
        link_rhs = (own_slab - summed).astype(BF16)
        partial_value = jnp.dot(link_rhs, link_inverse, preferred_element_type=F32)
        own_part = lax.psum(partial_value, "sec").astype(BF16)
        linking = lax.all_gather(own_part, "dev", axis=1, tiled=True)
        picked = jnp.einsum(
            "cqr,sq->csr", linking.reshape(columns, panel_count, panel), selector,
            preferred_element_type=F32,
        )
        picked = picked.reshape(columns, pb * panel).astype(BF16)
        pushed = jnp.dot(picked, coupling, preferred_element_type=F32)
        reduced = (corrected.astype(F32) - pushed).astype(BF16)
        previous = apply_tiles(tile_inv, reduced).astype(BF16)
    width = link_size // lax.axis_size("dev")
    link_out = lax.dynamic_slice_in_dim(linking, lax.axis_index("dev") * width, width, 1)
    return previous[None], link_out


def per_device(n_sec, n_dev, *args):
    link_coupling, link_panels, link_scale = args[1], args[2], args[5]
    panel = link_coupling.shape[1] // link_panels.shape[1]
    panels = link_scale.shape[0] // panel
    fits = n_dev % 2 == 0 and panels % (n_sec * n_dev) == 0 and panels <= 128
    if fits and n_sec > 1 and link_coupling.shape[0] == 1:
        return fused(n_sec, n_dev, panels // (n_sec * n_dev), *args)
    return plain(*args)


def solution(mesh):
    in_specs = (
        P(("sec", "dev"), None, None, None),
        P(("sec", "dev"), None, None),
        P(("sec", "dev"), None),
        P(("sec", "dev"), None, None),
        P(("sec", "dev"), None),
        P(),
        P("sec", "dev"),
    )
    out_specs = (P(("sec", "dev"), None, None), P(None, "dev"))
    body = functools.partial(per_device, mesh.shape["sec"], mesh.shape["dev"])
    return jax.shard_map(
        body, mesh=mesh, in_specs=in_specs, out_specs=out_specs, check_vma=False
    )
```

```python
import functools

import jax
import jax.numpy as jnp
from jax import lax
from jax.experimental import pallas as pl
from jax.experimental.pallas import tpu as pltpu
from jax.sharding import PartitionSpec as P

SOLVES = 5
F32 = jnp.float32
BF16 = jnp.bfloat16


def nn(a, b):
    return lax.dot_general(a, b, (((1,), (0,)), ((), ())), preferred_element_type=F32)


def nt(a, b):
    return lax.dot_general(a, b, (((1,), (1,)), ((), ())), preferred_element_type=F32)


PER_GROUP = 7
SEMS = 18


def kernel(n_sec, n_dev, per, groups, *refs):
    (panels_ref, tile_hbm, coup_hbm, rhs_hbm, scale_hbm, lscale_hbm, linv_hbm,
     leaf_out, link_out,
     tile_ref, coup_ref, rhs_ref, scale_ref, lscale_ref, linv, slot_v, slot_s,
     mmat, qmat, kmat, kacc, base, solved, umat, picked, part,
     in_sem, slot_sem, slot_send, slot_recv) = refs[:30]
    rest = refs[30:]
    span = PER_GROUP + SEMS
    buffers = [rest[g * span:g * span + PER_GROUP] for g in range(len(groups))]
    sems = [rest[g * span + PER_GROUP:(g + 1) * span] for g in range(len(groups))]
    n_groups = range(len(groups))
    s = lax.axis_index("sec")
    d = lax.axis_index("dev")
    n_z = n_dev // 2
    z = d // 2
    c = d % 2
    partner = z * 2 + (1 - c)
    pb = panels_ref.shape[1]
    tiles, tile = tile_ref.shape[0], tile_ref.shape[1]
    panel = coup_ref.shape[0] // pb
    per_sec = n_dev * per
    per_dev = n_sec * per
    own_rhs = s * per_sec + d * per

    def remote(src, send, recv, target, dst=None):
        return pltpu.make_async_remote_copy(
            src_ref=src, dst_ref=src if dst is None else dst, send_sem=send, recv_sem=recv,
            device_id=target, device_id_type=pl.DeviceIdType.MESH,
        )

    def started(copies):
        for copy in copies:
            copy.start()
        return copies

    def on_z(j, core):
        return ((z - j + n_z) % n_z) * 2 + core

    def rows(g):
        return pl.ds(groups[g][0], groups[g][1])

    loads = []

    def load(src, dst):
        copy = pltpu.make_async_copy(src, dst, in_sem.at[len(loads)])
        copy.start()
        loads.append(copy)
        return copy

    rhs_load = load(rhs_hbm, rhs_ref)
    coup_load = load(coup_hbm, coup_ref)
    tile_loads = [load(tile_hbm.at[t], tile_ref.at[t]) for t in range(tiles)]
    scale_load = load(scale_hbm, scale_ref)
    lscale_load = load(lscale_hbm, lscale_ref)
    linv_load = load(linv_hbm, linv)

    barrier = pltpu.get_barrier_semaphore()
    for j in range(1, n_dev):
        pl.semaphore_signal(barrier, inc=1, device_id={"dev": (d + j) % n_dev},
                            device_id_type=pl.DeviceIdType.MESH)
    for j in range(1, n_sec):
        pl.semaphore_signal(barrier, inc=1, device_id={"sec": (s + j) % n_sec},
                            device_id_type=pl.DeviceIdType.MESH)

    for g in n_groups:
        tbuf, link = buffers[g][0], buffers[g][6]
        zero_panel = jnp.zeros(tbuf.shape[3:], BF16)
        for k in range(SOLVES):
            for i in range(n_dev):
                tbuf[k, i, pb] = zero_panel
        for j in range(per):
            link[0, own_rhs + j] = zero_panel
    lane = lax.broadcasted_iota(jnp.int32, slot_v.shape[1:], 1)
    slots = jnp.full(slot_v.shape[1:], pb, jnp.int32)
    for q in range(pb):
        slots = jnp.where(lane == panels_ref[0, q], q, slots)
    slot_v[d] = slots

    rhs_load.wait()
    first = None
    for t in range(tiles):
        cols = pl.ds(t * tile, tile)
        tile_loads[t].wait()
        value = nt(rhs_ref[:, cols], tile_ref[t])
        solved[:, cols] = value
        if t == 0:
            coup_load.wait()
        term = nt(value.astype(BF16), coup_ref[:, cols])
        first = term if first is None else first + term
    base[...] = first

    pl.semaphore_wait(barrier, n_dev - 1 + n_sec - 1)

    slot_copies = started([
        remote(slot_v.at[d], slot_send.at[j], slot_recv.at[j], {"dev": (d + j) % n_dev})
        for j in range(1, n_dev)
    ])

    def along_z(ref, send, recv):
        return [remote(ref, send.at[j], recv.at[j], {"dev": ((z + j) % n_z) * 2 + c})
                for j in range(1, n_z)]

    def to_core(ref, send, recv, j):
        return remote(ref, send.at[j], recv.at[j], {"dev": partner})

    def touched_first(g, k):
        mine = buffers[g][0].at[k, d, pl.ds(0, pb)]
        return (along_z(mine, sems[g][0], sems[g][1])
                + [to_core(mine, sems[g][2], sems[g][3], 0)])

    def store_touched(g, k, value):
        for q in range(pb):
            buffers[g][0][k, d, q] = value[:, q * panel:(q + 1) * panel].astype(BF16)
        started(touched_first(g, k))

    for g in n_groups:
        store_touched(g, 0, base[rows(g), :])
    scale_load.wait()
    lscale_load.wait()

    def solve(k, carry):
        sends = []
        t_sends = []

        @pl.when(k == 0)
        def _():
            for t in range(tiles):
                cols = pl.ds(t * tile, tile)
                mmat[:, cols] = nn(coup_ref[:, cols], tile_ref[t]).astype(BF16)
                qmat[:, cols] = nt(coup_ref[:, cols], tile_ref[t]).astype(BF16)
            for copy in slot_copies:
                copy.wait()
            to_smem = pltpu.make_async_copy(slot_v, slot_s, slot_sem)
            to_smem.start()
            to_smem.wait()

        @pl.when(k > 0)
        def _():
            for t in range(tiles):
                cols = pl.ds(t * tile, tile)
                leaf = solved[:, cols] - nn(picked[...], qmat[:, cols])
                x = rhs_ref[:, cols].astype(F32) - scale_ref[:, cols] * leaf
                solved[:, cols] = nt(x.astype(BF16), tile_ref[t])

        r_copies = []
        for g in n_groups:
            tbuf, rsend, rrecv = buffers[g][0], buffers[g][1], buffers[g][2]
            copies = touched_first(g, k)
            cores = [copies[-1]]
            for j in range(1, n_z):
                copies[j - 1].wait_recv()
                piece = tbuf.at[k, on_z(j, c), pl.ds(0, pb)]
                cores += started([to_core(piece, sems[g][2], sems[g][3], j)])
            for copy in cores:
                copy.wait_recv()
            t_sends += copies[:-1] + cores
            for a in range(n_sec):
                for j in range(per):
                    q = a * per_sec + d * per + j
                    total = tbuf[k, 0, slot_s[0, 0, q]].astype(F32)
                    for i in range(1, n_dev):
                        total = total + tbuf[k, i, slot_s[i, 0, q]].astype(F32)
                    rsend[k, a, j] = total.astype(BF16)
            r_copies.append(started([
                remote(rsend.at[k, (s + j) % n_sec], sems[g][4].at[j], sems[g][5].at[j],
                       {"sec": (s + j) % n_sec}, rrecv.at[k, s])
                for j in range(1, n_sec)
            ]))
            sends += r_copies[g]

        def rhs_first(g):
            mine = buffers[g][3].at[k, d]
            return (along_z(mine, sems[g][6], sems[g][7])
                    + [to_core(mine, sems[g][8], sems[g][9], 0)])

        h_copies = []
        for g in n_groups:
            _, rsend, rrecv, hbuf, _, _, link = buffers[g]
            totals = []
            for j in range(per):
                prev = link[k, own_rhs + j].astype(F32)
                totals.append(-lscale_ref[pl.ds(own_rhs + j, 1), :] * prev
                              - rsend[k, s, j].astype(F32))
            for copy in r_copies[g]:
                copy.wait_recv()
            for j in range(per):
                total = totals[j]
                for i in range(1, n_sec):
                    total = total - rrecv[k, (s + i) % n_sec, j].astype(F32)
                hbuf[k, d, j] = total.astype(BF16)
            h_copies.append(started(rhs_first(g)))

        @pl.when(k == 0)
        def _():
            linv_load.wait()

        def multiply(g, owner):
            hbuf = buffers[g][3]
            left = jnp.concatenate([hbuf[k, owner, j] for j in range(per)], axis=1)
            depth = per * panel
            return nn(left, linv[pl.ds(pl.multiple_of(owner * depth, depth), depth), :])

        for g in n_groups:
            part[rows(g), :] = multiply(g, d)

        @pl.when(k < SOLVES - 1)
        def _():
            total = base[...]
            for t in range(tiles):
                cols = pl.ds(t * tile, tile)
                scaled = (scale_ref[:, cols] * solved[:, cols]).astype(BF16)
                total = total - nt(scaled, mmat[:, cols])
            umat[...] = total

        l_copies = []
        for g in n_groups:
            hbuf, lsend, lrecv = buffers[g][3], buffers[g][4], buffers[g][5]
            copies = h_copies[g]
            cores = [copies[-1]]
            for j in range(1, n_z):
                copies[j - 1].wait_recv()
                owner = on_z(j, c)
                cores += started([to_core(hbuf.at[k, owner], sems[g][8], sems[g][9], j)])
                part[rows(g), :] += multiply(g, owner)
            for j in range(n_z):
                cores[j].wait_recv()
                part[rows(g), :] += multiply(g, on_z(j, 1 - c))
            sends += copies[:-1] + cores
            for q in range(per_dev):
                lsend[k, q] = part[rows(g), q * panel:(q + 1) * panel].astype(BF16)
            l_copies.append(started([
                remote(lsend.at[k, pl.ds(((s + j) % n_sec) * per, per)],
                       sems[g][10].at[j], sems[g][11].at[j],
                       {"sec": (s + j) % n_sec}, lrecv.at[k, s])
                for j in range(1, n_sec)
            ]))
            sends += l_copies[g]

        @pl.when(k == 0)
        def _():
            for t in range(tiles):
                cols = pl.ds(t * tile, tile)
                scaled = (scale_ref[:, cols] * qmat[:, cols].astype(F32)).astype(BF16)
                term = nt(scaled, mmat[:, cols])
                if t == 0:
                    kacc[...] = term
                else:
                    kacc[...] += term
            kmat[...] = kacc[...].astype(BF16)

        def piece(g, owner, section):
            return buffers[g][6].at[k + 1, pl.ds(owner * per_dev + section * per, per)]

        z_copies = []
        for g in n_groups:
            lrecv, link = buffers[g][5], buffers[g][6]
            for copy in l_copies[g]:
                copy.wait_recv()
            for j in range(per):
                own_cols = pl.ds(pl.multiple_of((s * per + j) * panel, panel), panel)
                total = part[rows(g), own_cols]
                for i in range(1, n_sec):
                    total = total + lrecv[k, (s + i) % n_sec, j].astype(F32)
                link[k + 1, d * per_dev + s * per + j] = total.astype(BF16)
            z_copies.append(started(along_z(piece(g, d, s), sems[g][12], sems[g][13])))
            sends += z_copies[g]
        g_copies = []
        for g in n_groups:
            g_copies.append([])
            for i in range(n_z):
                if i > 0:
                    z_copies[g][i - 1].wait_recv()
                g_copies[g].append(started([
                    remote(piece(g, on_z(i, c), s), sems[g][14].at[i, j], sems[g][15].at[i, j],
                           {"sec": (s + j) % n_sec})
                    for j in range(1, n_sec)
                ]))
                sends += g_copies[g][i]
        c_copies = []
        for g in n_groups:
            c_copies.append([])
            for i in range(n_z):
                for copy in g_copies[g][i]:
                    copy.wait_recv()
                whole = buffers[g][6].at[k + 1, pl.ds(on_z(i, c) * per_dev, per_dev)]
                c_copies[g] += started([to_core(whole, sems[g][16], sems[g][17], i)])
            sends += c_copies[g]
        for copy in t_sends:
            copy.wait_send()
        for g in n_groups:
            for copy in c_copies[g]:
                copy.wait_recv()
            for q in range(pb):
                picked[rows(g), q * panel:(q + 1) * panel] = buffers[g][6][k + 1, panels_ref[0, q]]

            @pl.when(k < SOLVES - 1)
            def _():
                store_touched(g, k + 1, umat[rows(g), :] + nn(picked[rows(g), :], kmat[...]))

        for copy in sends:
            copy.wait_send()
        return carry

    lax.fori_loop(0, SOLVES, solve, 0)

    for t in range(tiles):
        cols = pl.ds(t * tile, tile)
        leaf_out[:, cols] = (solved[:, cols] - nn(picked[...], qmat[:, cols])).astype(BF16)
    for g in n_groups:
        for q in range(per_dev):
            link_out[rows(g), q * panel:(q + 1) * panel] = buffers[g][6][SOLVES, d * per_dev + q]


def row_groups(cols):
    if cols % 16 or cols < 32:
        return ((0, cols),)
    first = (cols // 16 + 1) // 2 * 16
    return ((0, first), (first, cols - first))


def fused(n_sec, n_dev, per, tile_inverse, link_coupling, link_panels, leaf_rhs, leaf_scale,
          link_scale, link_inverse):
    pb = link_panels.shape[1]
    rows, nb = link_coupling.shape[1:]
    panel = rows // pb
    cols = leaf_rhs.shape[1]
    total_panels = link_scale.shape[0] // panel
    per_dev = n_sec * per
    n_z = n_dev // 2
    groups = row_groups(cols)
    vmem = pl.BlockSpec(memory_space=pltpu.VMEM)
    dma = pltpu.SemaphoreType.DMA
    scratch = [
        pltpu.VMEM(tile_inverse.shape[1:], BF16),
        pltpu.VMEM((rows, nb), BF16),
        pltpu.VMEM((cols, nb), BF16),
        pltpu.VMEM((1, nb), F32),
        pltpu.VMEM((total_panels, panel), F32),
        pltpu.VMEM(link_inverse.shape, BF16),
        pltpu.VMEM((n_dev, 8, 128), jnp.int32),
        pltpu.SMEM((n_dev, 8, 128), jnp.int32),
        pltpu.VMEM((rows, nb), BF16),
        pltpu.VMEM((rows, nb), BF16),
        pltpu.VMEM((rows, rows), BF16),
        pltpu.VMEM((rows, rows), F32),
        pltpu.VMEM((cols, rows), F32),
        pltpu.VMEM((cols, nb), F32),
        pltpu.VMEM((cols, rows), F32),
        pltpu.VMEM((cols, rows), BF16),
        pltpu.VMEM((cols, per_dev * panel), F32),
        dma((tile_inverse.shape[1] + 5,)), dma, dma((n_dev,)), dma((n_dev,)),
    ]
    for _, size in groups:
        scratch += [
            pltpu.VMEM((SOLVES, n_dev, pb + 1, size, panel), BF16),
            pltpu.VMEM((SOLVES, n_sec, per, size, panel), BF16),
            pltpu.VMEM((SOLVES, n_sec, per, size, panel), BF16),
            pltpu.VMEM((SOLVES, n_dev, per, size, panel), BF16),
            pltpu.VMEM((SOLVES, per_dev, size, panel), BF16),
            pltpu.VMEM((SOLVES, n_sec, per, size, panel), BF16),
            pltpu.VMEM((SOLVES + 1, total_panels, size, panel), BF16),
        ]
        for shape in ((n_z,), (n_z,), (n_sec,), (n_z,), (n_z,), (n_sec,), (n_z,),
                      (n_z, n_sec), (n_z,)):
            scratch += [dma(shape), dma(shape)]
    leaf, link = pl.pallas_call(
        functools.partial(kernel, n_sec, n_dev, per, groups),
        out_shape=(
            jax.ShapeDtypeStruct((cols, nb), BF16),
            jax.ShapeDtypeStruct((cols, per_dev * panel), BF16),
        ),
        in_specs=[pl.BlockSpec(memory_space=pltpu.SMEM)]
        + [pl.BlockSpec(memory_space=pl.ANY)] * 6,
        out_specs=(vmem, vmem),
        scratch_shapes=scratch,
        compiler_params=pltpu.CompilerParams(
            collective_id=0, has_side_effects=True, vmem_limit_bytes=56 * 1024 * 1024
        ),
    )(
        link_panels, tile_inverse[0], link_coupling[0], leaf_rhs[0], leaf_scale,
        link_scale.reshape(total_panels, panel), link_inverse,
    )
    return leaf[None], link


def apply_tiles(tile_inv, vectors):
    columns = vectors.shape[0]
    blocked = vectors.reshape(columns, tile_inv.shape[0], tile_inv.shape[1])
    result = jnp.einsum("tab,ctb->cta", tile_inv, blocked, preferred_element_type=F32)
    return result.reshape(columns, -1)


def plain(tile_inverse, link_coupling, link_panels, leaf_rhs, leaf_scale, link_scale, link_inverse):
    tile_inv, coupling, leaf_gain = tile_inverse[0], link_coupling[0], leaf_scale[0]
    own_panels = link_panels[0]
    pb = own_panels.shape[0]
    panel = coupling.shape[0] // pb
    link_size = link_scale.shape[0]
    panel_count = link_size // panel
    matches = own_panels[:, None] == jnp.arange(panel_count, dtype=jnp.int32)[None, :]
    selector = matches.astype(BF16)
    spreader = matches.astype(F32)
    columns = leaf_rhs.shape[1]
    previous = jnp.zeros(leaf_rhs.shape[1:], BF16)
    linking = jnp.zeros((columns, link_size), BF16)
    for solve_index in range(SOLVES):
        corrected = leaf_rhs[0].astype(F32) - leaf_gain[None, :] * previous.astype(F32)
        corrected = corrected.astype(BF16)
        link_side = -link_scale[None, :] * linking.astype(F32)
        solved = apply_tiles(tile_inv, corrected).astype(BF16)
        touched = jnp.einsum("cn,rn->cr", solved, coupling, preferred_element_type=F32)
        touched = touched.reshape(columns, pb, panel)
        spread = jnp.einsum("csr,sq->cqr", touched, spreader).reshape(columns, link_size)
        section = lax.psum_scatter(
            spread.astype(BF16), "sec", scatter_dimension=1, tiled=True
        ).astype(F32)
        summed = lax.psum(section, "dev")
        width = summed.shape[1]
        own_slab = lax.dynamic_slice_in_dim(link_side, lax.axis_index("sec") * width, width, 1)
        link_rhs = (own_slab - summed).astype(BF16)
        partial_value = jnp.dot(link_rhs, link_inverse, preferred_element_type=F32)
        own_part = lax.psum(partial_value, "sec").astype(BF16)
        linking = lax.all_gather(own_part, "dev", axis=1, tiled=True)
        picked = jnp.einsum(
            "cqr,sq->csr", linking.reshape(columns, panel_count, panel), selector,
            preferred_element_type=F32,
        )
        picked = picked.reshape(columns, pb * panel).astype(BF16)
        pushed = jnp.dot(picked, coupling, preferred_element_type=F32)
        reduced = (corrected.astype(F32) - pushed).astype(BF16)
        previous = apply_tiles(tile_inv, reduced).astype(BF16)
    width = link_size // lax.axis_size("dev")
    link_out = lax.dynamic_slice_in_dim(linking, lax.axis_index("dev") * width, width, 1)
    return previous[None], link_out


def per_device(n_sec, n_dev, *args):
    link_coupling, link_panels, link_scale = args[1], args[2], args[5]
    panel = link_coupling.shape[1] // link_panels.shape[1]
    panels = link_scale.shape[0] // panel
    fits = n_dev % 2 == 0 and panels % (n_sec * n_dev) == 0 and panels <= 128
    if fits and n_sec > 1 and link_coupling.shape[0] == 1:
        return fused(n_sec, n_dev, panels // (n_sec * n_dev), *args)
    return plain(*args)


def solution(mesh):
    in_specs = (
        P(("sec", "dev"), None, None, None),
        P(("sec", "dev"), None, None),
        P(("sec", "dev"), None),
        P(("sec", "dev"), None, None),
        P(("sec", "dev"), None),
        P(),
        P("sec", "dev"),
    )
    out_specs = (P(("sec", "dev"), None, None), P(None, "dev"))
    body = functools.partial(per_device, mesh.shape["sec"], mesh.shape["dev"])
    return jax.shard_map(
        body, mesh=mesh, in_specs=in_specs, out_specs=out_specs, check_vma=False
    )
```

```python
import functools

import jax
import jax.numpy as jnp
from jax import lax
from jax.experimental import pallas as pl
from jax.experimental.pallas import tpu as pltpu
from jax.sharding import PartitionSpec as P

SOLVES = 5
F32 = jnp.float32
BF16 = jnp.bfloat16


def nn(a, b):
    return lax.dot_general(a, b, (((1,), (0,)), ((), ())), preferred_element_type=F32)


def nt(a, b):
    return lax.dot_general(a, b, (((1,), (1,)), ((), ())), preferred_element_type=F32)


PER_GROUP = 7
SEMS = 14


def kernel(n_sec, n_dev, per, groups, *refs):
    (panels_ref, tile_hbm, coup_hbm, rhs_hbm, scale_hbm, lscale_hbm, linv_hbm,
     leaf_out, link_out,
     tile_ref, coup_ref, rhs_ref, scale_ref, lscale_ref, wown, wother, slot_v, slot_s,
     mmat, qmat, kmat, kacc, base, solved, umat, picked, part,
     in_sem, slot_sem, slot_send, slot_recv, w_send, w_recv) = refs[:33]
    rest = refs[33:]
    span = PER_GROUP + SEMS
    buffers = [rest[g * span:g * span + PER_GROUP] for g in range(len(groups))]
    sems = [rest[g * span + PER_GROUP:(g + 1) * span] for g in range(len(groups))]
    n_groups = range(len(groups))
    s = lax.axis_index("sec")
    d = lax.axis_index("dev")
    n_z = n_dev // 2
    z = d // 2
    c = d % 2
    partner = z * 2 + (1 - c)
    pb = panels_ref.shape[1]
    tiles, tile = tile_ref.shape[0], tile_ref.shape[1]
    panel = coup_ref.shape[0] // pb
    per_sec = n_dev * per
    per_dev = n_sec * per
    own_rhs = s * per_sec + d * per

    def remote(src, send, recv, target, dst=None):
        return pltpu.make_async_remote_copy(
            src_ref=src, dst_ref=src if dst is None else dst, send_sem=send, recv_sem=recv,
            device_id=target, device_id_type=pl.DeviceIdType.MESH,
        )

    def started(copies):
        for copy in copies:
            copy.start()
        return copies

    def on_z(j, core):
        return ((z - j + n_z) % n_z) * 2 + core

    def rows(g):
        return pl.ds(groups[g][0], groups[g][1])

    loads = []

    def load(src, dst):
        copy = pltpu.make_async_copy(src, dst, in_sem.at[len(loads)])
        copy.start()
        loads.append(copy)
        return copy

    rhs_load = load(rhs_hbm, rhs_ref)
    coup_load = load(coup_hbm, coup_ref)
    tile_loads = [load(tile_hbm.at[t], tile_ref.at[t]) for t in range(tiles)]
    scale_load = load(scale_hbm, scale_ref)
    lscale_load = load(lscale_hbm, lscale_ref)

    def inverse_rows(owner):
        depth = per * panel
        return linv_hbm.at[pl.ds(pl.multiple_of(owner * depth, depth), depth)]

    w_loads = [load(inverse_rows(i * 2 + c), wown.at[i]) for i in range(n_z)]

    barrier = pltpu.get_barrier_semaphore()
    def at_z(m):
        return {"sec": (s + m // 2) % n_sec, "dev": z * 2 + (c + m % 2) % 2}

    n_at_z = 2 * n_sec
    for j in range(1, n_z):
        pl.semaphore_signal(barrier, inc=1, device_id={"dev": on_z(j, c)},
                            device_id_type=pl.DeviceIdType.MESH)
    for m in range(1, n_at_z):
        pl.semaphore_signal(barrier, inc=1, device_id=at_z(m),
                            device_id_type=pl.DeviceIdType.MESH)

    for g in n_groups:
        tbuf, link = buffers[g][0], buffers[g][6]
        zero_panel = jnp.zeros(tbuf.shape[3:], BF16)
        for k in range(SOLVES):
            for i in range(n_z):
                tbuf[k, i, pb] = zero_panel
        for j in range(per):
            link[0, own_rhs + j] = zero_panel
    lane = lax.broadcasted_iota(jnp.int32, slot_v.shape[1:], 1)
    slots = jnp.full(slot_v.shape[1:], pb, jnp.int32)
    for q in range(pb):
        slots = jnp.where(lane == panels_ref[0, q], q, slots)
    slot_v[z] = slots

    rhs_load.wait()
    first = None
    for t in range(tiles):
        cols = pl.ds(t * tile, tile)
        tile_loads[t].wait()
        value = nt(rhs_ref[:, cols], tile_ref[t])
        solved[:, cols] = value
        if t == 0:
            coup_load.wait()
        term = nt(value.astype(BF16), coup_ref[:, cols])
        first = term if first is None else first + term
    base[...] = first

    pl.semaphore_wait(barrier, n_z - 1 + n_at_z - 1)

    def along_z(ref, send, recv):
        return [remote(ref, send.at[j], recv.at[j], {"dev": ((z + j) % n_z) * 2 + c})
                for j in range(1, n_z)]

    def to_core(ref, send, recv, j):
        return remote(ref, send.at[j], recv.at[j], {"dev": partner})

    def touched_sends(g, k):
        return along_z(buffers[g][0].at[k, z, pl.ds(0, pb)], sems[g][0], sems[g][1])

    def store_touched(g, k, value):
        for q in range(pb):
            buffers[g][0][k, z, q] = value[:, q * panel:(q + 1) * panel].astype(BF16)
        started(touched_sends(g, k))

    for g in n_groups:
        store_touched(g, 0, base[rows(g), :])
    slot_copies = started(along_z(slot_v.at[z], slot_send, slot_recv))
    w_copies = started([
        remote(inverse_rows(i * 2 + 1 - c), w_send.at[i], w_recv.at[i], {"dev": partner},
               wother.at[i])
        for i in range(n_z)
    ])
    scale_load.wait()
    lscale_load.wait()

    def solve(k, carry):
        sends = []
        t_sends = []

        @pl.when(k == 0)
        def _():
            for t in range(tiles):
                cols = pl.ds(t * tile, tile)
                mmat[:, cols] = nn(coup_ref[:, cols], tile_ref[t]).astype(BF16)
                qmat[:, cols] = nt(coup_ref[:, cols], tile_ref[t]).astype(BF16)
            for copy in slot_copies:
                copy.wait()
            to_smem = pltpu.make_async_copy(slot_v, slot_s, slot_sem)
            to_smem.start()
            to_smem.wait()

        @pl.when(k > 0)
        def _():
            for t in range(tiles):
                cols = pl.ds(t * tile, tile)
                leaf = solved[:, cols] - nn(picked[...], qmat[:, cols])
                x = rhs_ref[:, cols].astype(F32) - scale_ref[:, cols] * leaf
                solved[:, cols] = nt(x.astype(BF16), tile_ref[t])

        r_copies = []
        for g in n_groups:
            tbuf, rsend, rrecv = buffers[g][0], buffers[g][1], buffers[g][2]
            copies = touched_sends(g, k)
            for copy in copies:
                copy.wait_recv()
            t_sends += copies
            for a in range(n_sec):
                for b in range(2):
                    for j in range(per):
                        q = a * per_sec + (z * 2 + b) * per + j
                        total = tbuf[k, 0, slot_s[0, 0, q]].astype(F32)
                        for i in range(1, n_z):
                            total = total + tbuf[k, i, slot_s[i, 0, q]].astype(F32)
                        rsend[k, a, b, j] = total.astype(BF16)
            r_copies.append(started([
                remote(rsend.at[k, (s + m // 2) % n_sec, (c + m % 2) % 2], sems[g][2].at[m],
                       sems[g][3].at[m], at_z(m), rrecv.at[k, m])
                for m in range(1, n_at_z)
            ]))
            sends += r_copies[g]

        h_copies = []
        for g in n_groups:
            _, rsend, rrecv, hbuf, _, _, link = buffers[g]
            totals = []
            for j in range(per):
                prev = link[k, own_rhs + j].astype(F32)
                totals.append(-lscale_ref[pl.ds(own_rhs + j, 1), :] * prev
                              - rsend[k, s, c, j].astype(F32))
            for copy in r_copies[g]:
                copy.wait_recv()
            for j in range(per):
                total = totals[j]
                for m in range(1, n_at_z):
                    total = total - rrecv[k, m, j].astype(F32)
                hbuf[k, z, j] = total.astype(BF16)
            h_copies.append(started(along_z(hbuf.at[k, z], sems[g][4], sems[g][5])))

        @pl.when(k == 0)
        def _():
            for copy in w_loads + w_copies:
                copy.wait()

        def multiply(g, owner):
            hbuf = buffers[g][3]
            left = jnp.concatenate([hbuf[k, owner, j] for j in range(per)], axis=1)
            return nn(left, wown[owner]), nn(left, wother[owner])

        half = per_dev * panel

        for g in n_groups:
            part[rows(g), :half], part[rows(g), half:] = multiply(g, z)

        @pl.when(k < SOLVES - 1)
        def _():
            total = base[...]
            for t in range(tiles):
                cols = pl.ds(t * tile, tile)
                scaled = (scale_ref[:, cols] * solved[:, cols]).astype(BF16)
                total = total - nt(scaled, mmat[:, cols])
            umat[...] = total

        l_copies = []
        for g in n_groups:
            hbuf, lsend, lrecv = buffers[g][3], buffers[g][4], buffers[g][5]
            copies = h_copies[g]
            for j in range(1, n_z):
                copies[j - 1].wait_recv()
                near, far = multiply(g, (z - j + n_z) % n_z)
                part[rows(g), :half] += near
                part[rows(g), half:] += far
            sends += copies
            for b in range(2):
                for q in range(per_dev):
                    at = b * half + q * panel
                    lsend[k, b, q] = part[rows(g), at:at + panel].astype(BF16)
            l_copies.append(started([
                remote(lsend.at[k, m % 2, pl.ds(((s + m // 2) % n_sec) * per, per)],
                       sems[g][6].at[m], sems[g][7].at[m], at_z(m), lrecv.at[k, m])
                for m in range(1, n_at_z)
            ]))
            sends += l_copies[g]

        @pl.when(k == 0)
        def _():
            for t in range(tiles):
                cols = pl.ds(t * tile, tile)
                scaled = (scale_ref[:, cols] * qmat[:, cols].astype(F32)).astype(BF16)
                term = nt(scaled, mmat[:, cols])
                if t == 0:
                    kacc[...] = term
                else:
                    kacc[...] += term
            kmat[...] = kacc[...].astype(BF16)

        def piece(g, owner, section):
            return buffers[g][6].at[k + 1, pl.ds(owner * per_dev + section * per, per)]

        z_copies = []
        for g in n_groups:
            lrecv, link = buffers[g][5], buffers[g][6]
            for copy in l_copies[g]:
                copy.wait_recv()
            for j in range(per):
                own_cols = pl.ds(pl.multiple_of((s * per + j) * panel, panel), panel)
                total = part[rows(g), own_cols]
                for m in range(1, n_at_z):
                    total = total + lrecv[k, m, j].astype(F32)
                link[k + 1, d * per_dev + s * per + j] = total.astype(BF16)
            z_copies.append(started(along_z(piece(g, d, s), sems[g][8], sems[g][9])))
            sends += z_copies[g]
        g_copies = []
        for g in n_groups:
            g_copies.append([])
            for i in range(n_z):
                if i > 0:
                    z_copies[g][i - 1].wait_recv()
                g_copies[g].append(started([
                    remote(piece(g, on_z(i, c), s), sems[g][10].at[i, j], sems[g][11].at[i, j],
                           {"sec": (s + j) % n_sec})
                    for j in range(1, n_sec)
                ]))
                sends += g_copies[g][i]
        c_copies = []
        for g in n_groups:
            c_copies.append([])
            for i in range(n_z):
                for copy in g_copies[g][i]:
                    copy.wait_recv()
                whole = buffers[g][6].at[k + 1, pl.ds(on_z(i, c) * per_dev, per_dev)]
                c_copies[g] += started([to_core(whole, sems[g][12], sems[g][13], i)])
            sends += c_copies[g]
        for copy in t_sends:
            copy.wait_send()
        for g in n_groups:
            for copy in c_copies[g]:
                copy.wait_recv()
            for q in range(pb):
                picked[rows(g), q * panel:(q + 1) * panel] = buffers[g][6][k + 1, panels_ref[0, q]]

            @pl.when(k < SOLVES - 1)
            def _():
                store_touched(g, k + 1, umat[rows(g), :] + nn(picked[rows(g), :], kmat[...]))

        for copy in sends:
            copy.wait_send()
        return carry

    lax.fori_loop(0, SOLVES, solve, 0)

    for t in range(tiles):
        cols = pl.ds(t * tile, tile)
        leaf_out[:, cols] = (solved[:, cols] - nn(picked[...], qmat[:, cols])).astype(BF16)
    for g in n_groups:
        for q in range(per_dev):
            link_out[rows(g), q * panel:(q + 1) * panel] = buffers[g][6][SOLVES, d * per_dev + q]


def row_groups(cols):
    if cols % 16 or cols < 32:
        return ((0, cols),)
    first = (cols // 16 + 1) // 2 * 16
    return ((0, first), (first, cols - first))


def fused(n_sec, n_dev, per, tile_inverse, link_coupling, link_panels, leaf_rhs, leaf_scale,
          link_scale, link_inverse):
    pb = link_panels.shape[1]
    rows, nb = link_coupling.shape[1:]
    panel = rows // pb
    cols = leaf_rhs.shape[1]
    total_panels = link_scale.shape[0] // panel
    per_dev = n_sec * per
    n_z = n_dev // 2
    groups = row_groups(cols)
    vmem = pl.BlockSpec(memory_space=pltpu.VMEM)
    dma = pltpu.SemaphoreType.DMA
    scratch = [
        pltpu.VMEM(tile_inverse.shape[1:], BF16),
        pltpu.VMEM((rows, nb), BF16),
        pltpu.VMEM((cols, nb), BF16),
        pltpu.VMEM((1, nb), F32),
        pltpu.VMEM((total_panels, panel), F32),
        pltpu.VMEM((n_z, per * panel, per_dev * panel), BF16),
        pltpu.VMEM((n_z, per * panel, per_dev * panel), BF16),
        pltpu.VMEM((n_z, 8, 128), jnp.int32),
        pltpu.SMEM((n_z, 8, 128), jnp.int32),
        pltpu.VMEM((rows, nb), BF16),
        pltpu.VMEM((rows, nb), BF16),
        pltpu.VMEM((rows, rows), BF16),
        pltpu.VMEM((rows, rows), F32),
        pltpu.VMEM((cols, rows), F32),
        pltpu.VMEM((cols, nb), F32),
        pltpu.VMEM((cols, rows), F32),
        pltpu.VMEM((cols, rows), BF16),
        pltpu.VMEM((cols, 2 * per_dev * panel), F32),
        dma((tile_inverse.shape[1] + 4 + n_z,)), dma, dma((n_z,)), dma((n_z,)),
        dma((n_z,)), dma((n_z,)),
    ]
    for _, size in groups:
        scratch += [
            pltpu.VMEM((SOLVES, n_z, pb + 1, size, panel), BF16),
            pltpu.VMEM((SOLVES, n_sec, 2, per, size, panel), BF16),
            pltpu.VMEM((SOLVES, 2 * n_sec, per, size, panel), BF16),
            pltpu.VMEM((SOLVES, n_z, per, size, panel), BF16),
            pltpu.VMEM((SOLVES, 2, per_dev, size, panel), BF16),
            pltpu.VMEM((SOLVES, 2 * n_sec, per, size, panel), BF16),
            pltpu.VMEM((SOLVES + 1, total_panels, size, panel), BF16),
        ]
        for shape in ((n_z,), (2 * n_sec,), (n_z,), (2 * n_sec,), (n_z,), (n_z, n_sec), (n_z,)):
            scratch += [dma(shape), dma(shape)]
    leaf, link = pl.pallas_call(
        functools.partial(kernel, n_sec, n_dev, per, groups),
        out_shape=(
            jax.ShapeDtypeStruct((cols, nb), BF16),
            jax.ShapeDtypeStruct((cols, per_dev * panel), BF16),
        ),
        in_specs=[pl.BlockSpec(memory_space=pltpu.SMEM)]
        + [pl.BlockSpec(memory_space=pl.ANY)] * 6,
        out_specs=(vmem, vmem),
        scratch_shapes=scratch,
        compiler_params=pltpu.CompilerParams(
            collective_id=0, has_side_effects=True, vmem_limit_bytes=56 * 1024 * 1024
        ),
    )(
        link_panels, tile_inverse[0], link_coupling[0], leaf_rhs[0], leaf_scale,
        link_scale.reshape(total_panels, panel), link_inverse,
    )
    return leaf[None], link


def apply_tiles(tile_inv, vectors):
    columns = vectors.shape[0]
    blocked = vectors.reshape(columns, tile_inv.shape[0], tile_inv.shape[1])
    result = jnp.einsum("tab,ctb->cta", tile_inv, blocked, preferred_element_type=F32)
    return result.reshape(columns, -1)


def plain(tile_inverse, link_coupling, link_panels, leaf_rhs, leaf_scale, link_scale, link_inverse):
    tile_inv, coupling, leaf_gain = tile_inverse[0], link_coupling[0], leaf_scale[0]
    own_panels = link_panels[0]
    pb = own_panels.shape[0]
    panel = coupling.shape[0] // pb
    link_size = link_scale.shape[0]
    panel_count = link_size // panel
    matches = own_panels[:, None] == jnp.arange(panel_count, dtype=jnp.int32)[None, :]
    selector = matches.astype(BF16)
    spreader = matches.astype(F32)
    columns = leaf_rhs.shape[1]
    previous = jnp.zeros(leaf_rhs.shape[1:], BF16)
    linking = jnp.zeros((columns, link_size), BF16)
    for solve_index in range(SOLVES):
        corrected = leaf_rhs[0].astype(F32) - leaf_gain[None, :] * previous.astype(F32)
        corrected = corrected.astype(BF16)
        link_side = -link_scale[None, :] * linking.astype(F32)
        solved = apply_tiles(tile_inv, corrected).astype(BF16)
        touched = jnp.einsum("cn,rn->cr", solved, coupling, preferred_element_type=F32)
        touched = touched.reshape(columns, pb, panel)
        spread = jnp.einsum("csr,sq->cqr", touched, spreader).reshape(columns, link_size)
        section = lax.psum_scatter(
            spread.astype(BF16), "sec", scatter_dimension=1, tiled=True
        ).astype(F32)
        summed = lax.psum(section, "dev")
        width = summed.shape[1]
        own_slab = lax.dynamic_slice_in_dim(link_side, lax.axis_index("sec") * width, width, 1)
        link_rhs = (own_slab - summed).astype(BF16)
        partial_value = jnp.dot(link_rhs, link_inverse, preferred_element_type=F32)
        own_part = lax.psum(partial_value, "sec").astype(BF16)
        linking = lax.all_gather(own_part, "dev", axis=1, tiled=True)
        picked = jnp.einsum(
            "cqr,sq->csr", linking.reshape(columns, panel_count, panel), selector,
            preferred_element_type=F32,
        )
        picked = picked.reshape(columns, pb * panel).astype(BF16)
        pushed = jnp.dot(picked, coupling, preferred_element_type=F32)
        reduced = (corrected.astype(F32) - pushed).astype(BF16)
        previous = apply_tiles(tile_inv, reduced).astype(BF16)
    width = link_size // lax.axis_size("dev")
    link_out = lax.dynamic_slice_in_dim(linking, lax.axis_index("dev") * width, width, 1)
    return previous[None], link_out


def per_device(n_sec, n_dev, *args):
    link_coupling, link_panels, link_scale = args[1], args[2], args[5]
    panel = link_coupling.shape[1] // link_panels.shape[1]
    panels = link_scale.shape[0] // panel
    fits = n_dev % 2 == 0 and panels % (n_sec * n_dev) == 0 and panels <= 128
    if fits and n_sec > 1 and link_coupling.shape[0] == 1:
        return fused(n_sec, n_dev, panels // (n_sec * n_dev), *args)
    return plain(*args)


def solution(mesh):
    in_specs = (
        P(("sec", "dev"), None, None, None),
        P(("sec", "dev"), None, None),
        P(("sec", "dev"), None),
        P(("sec", "dev"), None, None),
        P(("sec", "dev"), None),
        P(),
        P("sec", "dev"),
    )
    out_specs = (P(("sec", "dev"), None, None), P(None, "dev"))
    body = functools.partial(per_device, mesh.shape["sec"], mesh.shape["dev"])
    return jax.shard_map(
        body, mesh=mesh, in_specs=in_specs, out_specs=out_specs, check_vma=False
    )
```

```python
import functools

import jax
import jax.numpy as jnp
from jax import lax
from jax.experimental import pallas as pl
from jax.experimental.pallas import tpu as pltpu
from jax.sharding import PartitionSpec as P

SOLVES = 5
F32 = jnp.float32
BF16 = jnp.bfloat16


def nn(a, b):
    return lax.dot_general(a, b, (((1,), (0,)), ((), ())), preferred_element_type=F32)


def nt(a, b):
    return lax.dot_general(a, b, (((1,), (1,)), ((), ())), preferred_element_type=F32)


PER_GROUP = 7
SEMS = 14


def kernel(n_sec, n_dev, per, groups, *refs):
    (panels_ref, tile_hbm, coup_hbm, rhs_hbm, scale_hbm, lscale_hbm, linv_hbm,
     leaf_out, link_out,
     tile_ref, coup_ref, rhs_ref, scale_ref, lscale_ref, wown, wother, slot_v, slot_s,
     tile_t, mmat, qmat, kmat, kacc, base, solved, umat, picked, part,
     in_sem, slot_sem, slot_send, slot_recv, w_send, w_recv) = refs[:34]
    rest = refs[34:]
    span = PER_GROUP + SEMS
    buffers = [rest[g * span:g * span + PER_GROUP] for g in range(len(groups))]
    sems = [rest[g * span + PER_GROUP:(g + 1) * span] for g in range(len(groups))]
    n_groups = range(len(groups))
    s = lax.axis_index("sec")
    d = lax.axis_index("dev")
    n_z = n_dev // 2
    z = d // 2
    c = d % 2
    partner = z * 2 + (1 - c)
    pb = panels_ref.shape[1]
    tiles, tile = tile_ref.shape[0], tile_ref.shape[1]
    panel = coup_ref.shape[0] // pb
    per_sec = n_dev * per
    per_dev = n_sec * per
    own_rhs = s * per_sec + d * per

    def remote(src, send, recv, target, dst=None):
        return pltpu.make_async_remote_copy(
            src_ref=src, dst_ref=src if dst is None else dst, send_sem=send, recv_sem=recv,
            device_id=target, device_id_type=pl.DeviceIdType.MESH,
        )

    def started(copies):
        for copy in copies:
            copy.start()
        return copies

    def on_z(j, core):
        return ((z - j + n_z) % n_z) * 2 + core

    def rows(g):
        return pl.ds(groups[g][0], groups[g][1])

    loads = []

    def load(src, dst):
        copy = pltpu.make_async_copy(src, dst, in_sem.at[len(loads)])
        copy.start()
        loads.append(copy)
        return copy

    rhs_load = load(rhs_hbm, rhs_ref)
    coup_load = load(coup_hbm, coup_ref)
    tile_loads = [load(tile_hbm.at[t], tile_ref.at[t]) for t in range(tiles)]
    scale_load = load(scale_hbm, scale_ref)
    lscale_load = load(lscale_hbm, lscale_ref)

    def inverse_rows(owner):
        depth = per * panel
        return linv_hbm.at[pl.ds(pl.multiple_of(owner * depth, depth), depth)]

    w_loads = [load(inverse_rows(i * 2 + c), wown.at[i]) for i in range(n_z)]

    barrier = pltpu.get_barrier_semaphore()
    def at_z(m):
        return {"sec": (s + m // 2) % n_sec, "dev": z * 2 + (c + m % 2) % 2}

    n_at_z = 2 * n_sec
    for j in range(1, n_z):
        pl.semaphore_signal(barrier, inc=1, device_id={"dev": on_z(j, c)},
                            device_id_type=pl.DeviceIdType.MESH)
    for m in range(1, n_at_z):
        pl.semaphore_signal(barrier, inc=1, device_id=at_z(m),
                            device_id_type=pl.DeviceIdType.MESH)

    for g in n_groups:
        tbuf, link = buffers[g][0], buffers[g][6]
        zero_panel = jnp.zeros(tbuf.shape[3:], BF16)
        for k in range(SOLVES):
            for i in range(n_z):
                tbuf[k, i, pb] = zero_panel
        for j in range(per):
            link[0, own_rhs + j] = zero_panel
    lane = lax.broadcasted_iota(jnp.int32, slot_v.shape[1:], 1)
    slots = jnp.full(slot_v.shape[1:], pb, jnp.int32)
    for q in range(pb):
        slots = jnp.where(lane == panels_ref[0, q], q, slots)
    slot_v[z] = slots

    rhs_load.wait()
    first = None
    for t in range(tiles):
        cols = pl.ds(t * tile, tile)
        tile_loads[t].wait()
        tile_t[t] = tile_ref[t].T
        value = nn(rhs_ref[:, cols], tile_t[t])
        solved[:, cols] = value
        if t == 0:
            coup_load.wait()
        term = nt(value.astype(BF16), coup_ref[:, cols])
        first = term if first is None else first + term
    base[...] = first

    pl.semaphore_wait(barrier, n_z - 1 + n_at_z - 1)

    def along_z(ref, send, recv):
        return [remote(ref, send.at[j], recv.at[j], {"dev": ((z + j) % n_z) * 2 + c})
                for j in range(1, n_z)]

    def to_core(ref, send, recv, j):
        return remote(ref, send.at[j], recv.at[j], {"dev": partner})

    def touched_sends(g, k):
        return along_z(buffers[g][0].at[k, z, pl.ds(0, pb)], sems[g][0], sems[g][1])

    def store_touched(g, k, value):
        for q in range(pb):
            buffers[g][0][k, z, q] = value[:, q * panel:(q + 1) * panel].astype(BF16)
        started(touched_sends(g, k))

    for g in n_groups:
        store_touched(g, 0, base[rows(g), :])
    slot_copies = started(along_z(slot_v.at[z], slot_send, slot_recv))
    w_copies = started([
        remote(inverse_rows(i * 2 + 1 - c), w_send.at[i], w_recv.at[i], {"dev": partner},
               wother.at[i])
        for i in range(n_z)
    ])
    scale_load.wait()
    lscale_load.wait()

    def solve(k, carry):
        sends = []
        t_sends = []

        @pl.when(k == 0)
        def _():
            for t in range(tiles):
                cols = pl.ds(t * tile, tile)
                mmat[cols, :] = nn(coup_ref[:, cols], tile_ref[t]).astype(BF16).T
                qmat[:, cols] = nn(coup_ref[:, cols], tile_t[t]).astype(BF16)
            for copy in slot_copies:
                copy.wait()
            to_smem = pltpu.make_async_copy(slot_v, slot_s, slot_sem)
            to_smem.start()
            to_smem.wait()

        @pl.when(k > 0)
        def _():
            for t in range(tiles):
                cols = pl.ds(t * tile, tile)
                leaf = solved[:, cols] - nn(picked[...], qmat[:, cols])
                x = rhs_ref[:, cols].astype(F32) - scale_ref[:, cols] * leaf
                solved[:, cols] = nn(x.astype(BF16), tile_t[t])

        r_copies = []
        for g in n_groups:
            tbuf, rsend, rrecv = buffers[g][0], buffers[g][1], buffers[g][2]
            copies = touched_sends(g, k)
            for copy in copies:
                copy.wait_recv()
            t_sends += copies
            for a in range(n_sec):
                for b in range(2):
                    for j in range(per):
                        q = a * per_sec + (z * 2 + b) * per + j
                        total = tbuf[k, 0, slot_s[0, 0, q]].astype(F32)
                        for i in range(1, n_z):
                            total = total + tbuf[k, i, slot_s[i, 0, q]].astype(F32)
                        rsend[k, a, b, j] = total.astype(BF16)
            r_copies.append(started([
                remote(rsend.at[k, (s + m // 2) % n_sec, (c + m % 2) % 2], sems[g][2].at[m],
                       sems[g][3].at[m], at_z(m), rrecv.at[k, m])
                for m in range(1, n_at_z)
            ]))
            sends += r_copies[g]

        h_copies = []
        for g in n_groups:
            _, rsend, rrecv, hbuf, _, _, link = buffers[g]
            totals = []
            for j in range(per):
                prev = link[k, own_rhs + j].astype(F32)
                totals.append(-lscale_ref[pl.ds(own_rhs + j, 1), :] * prev
                              - rsend[k, s, c, j].astype(F32))
            for copy in r_copies[g]:
                copy.wait_recv()
            for j in range(per):
                total = totals[j]
                for m in range(1, n_at_z):
                    total = total - rrecv[k, m, j].astype(F32)
                hbuf[k, z, j] = total.astype(BF16)
            h_copies.append(started(along_z(hbuf.at[k, z], sems[g][4], sems[g][5])))

        @pl.when(k == 0)
        def _():
            for copy in w_loads + w_copies:
                copy.wait()

        def multiply(g, owner):
            hbuf = buffers[g][3]
            left = jnp.concatenate([hbuf[k, owner, j] for j in range(per)], axis=1)
            return nn(left, wown[owner]), nn(left, wother[owner])

        half = per_dev * panel

        for g in n_groups:
            part[rows(g), :half], part[rows(g), half:] = multiply(g, z)

        @pl.when(k < SOLVES - 1)
        def _():
            total = base[...]
            for t in range(tiles):
                cols = pl.ds(t * tile, tile)
                scaled = (scale_ref[:, cols] * solved[:, cols]).astype(BF16)
                total = total - nn(scaled, mmat[cols, :])
            umat[...] = total

        l_copies = []
        for g in n_groups:
            hbuf, lsend, lrecv = buffers[g][3], buffers[g][4], buffers[g][5]
            copies = h_copies[g]
            for j in range(1, n_z):
                copies[j - 1].wait_recv()
                near, far = multiply(g, (z - j + n_z) % n_z)
                part[rows(g), :half] += near
                part[rows(g), half:] += far
            sends += copies
            for b in range(2):
                for q in range(per_dev):
                    at = b * half + q * panel
                    lsend[k, b, q] = part[rows(g), at:at + panel].astype(BF16)
            l_copies.append(started([
                remote(lsend.at[k, m % 2, pl.ds(((s + m // 2) % n_sec) * per, per)],
                       sems[g][6].at[m], sems[g][7].at[m], at_z(m), lrecv.at[k, m])
                for m in range(1, n_at_z)
            ]))
            sends += l_copies[g]

        @pl.when(k == 0)
        def _():
            for t in range(tiles):
                cols = pl.ds(t * tile, tile)
                scaled = (scale_ref[:, cols] * qmat[:, cols].astype(F32)).astype(BF16)
                term = nn(scaled, mmat[cols, :])
                if t == 0:
                    kacc[...] = term
                else:
                    kacc[...] += term
            kmat[...] = kacc[...].astype(BF16)

        def piece(g, owner, section):
            return buffers[g][6].at[k + 1, pl.ds(owner * per_dev + section * per, per)]

        z_copies = []
        for g in n_groups:
            lrecv, link = buffers[g][5], buffers[g][6]
            for copy in l_copies[g]:
                copy.wait_recv()
            for j in range(per):
                own_cols = pl.ds(pl.multiple_of((s * per + j) * panel, panel), panel)
                total = part[rows(g), own_cols]
                for m in range(1, n_at_z):
                    total = total + lrecv[k, m, j].astype(F32)
                link[k + 1, d * per_dev + s * per + j] = total.astype(BF16)
            z_copies.append(started(along_z(piece(g, d, s), sems[g][8], sems[g][9])))
            sends += z_copies[g]
        g_copies = []
        for g in n_groups:
            g_copies.append([])
            for i in range(n_z):
                if i > 0:
                    z_copies[g][i - 1].wait_recv()
                g_copies[g].append(started([
                    remote(piece(g, on_z(i, c), s), sems[g][10].at[i, j], sems[g][11].at[i, j],
                           {"sec": (s + j) % n_sec})
                    for j in range(1, n_sec)
                ]))
                sends += g_copies[g][i]
        c_copies = []
        for g in n_groups:
            c_copies.append([])
            for i in range(n_z):
                for copy in g_copies[g][i]:
                    copy.wait_recv()
                whole = buffers[g][6].at[k + 1, pl.ds(on_z(i, c) * per_dev, per_dev)]
                c_copies[g] += started([to_core(whole, sems[g][12], sems[g][13], i)])
            sends += c_copies[g]
        for copy in t_sends:
            copy.wait_send()
        for g in n_groups:
            for copy in c_copies[g]:
                copy.wait_recv()
            for q in range(pb):
                picked[rows(g), q * panel:(q + 1) * panel] = buffers[g][6][k + 1, panels_ref[0, q]]

            @pl.when(k < SOLVES - 1)
            def _():
                store_touched(g, k + 1, umat[rows(g), :] + nn(picked[rows(g), :], kmat[...]))

        for copy in sends:
            copy.wait_send()
        return carry

    lax.fori_loop(0, SOLVES, solve, 0)

    for t in range(tiles):
        cols = pl.ds(t * tile, tile)
        leaf_out[:, cols] = (solved[:, cols] - nn(picked[...], qmat[:, cols])).astype(BF16)
    for g in n_groups:
        for q in range(per_dev):
            link_out[rows(g), q * panel:(q + 1) * panel] = buffers[g][6][SOLVES, d * per_dev + q]


def row_groups(cols):
    if cols % 16 or cols < 32:
        return ((0, cols),)
    first = (cols // 16 + 1) // 2 * 16
    return ((0, first), (first, cols - first))


def fused(n_sec, n_dev, per, tile_inverse, link_coupling, link_panels, leaf_rhs, leaf_scale,
          link_scale, link_inverse):
    pb = link_panels.shape[1]
    rows, nb = link_coupling.shape[1:]
    panel = rows // pb
    cols = leaf_rhs.shape[1]
    total_panels = link_scale.shape[0] // panel
    per_dev = n_sec * per
    n_z = n_dev // 2
    groups = row_groups(cols)
    vmem = pl.BlockSpec(memory_space=pltpu.VMEM)
    dma = pltpu.SemaphoreType.DMA
    scratch = [
        pltpu.VMEM(tile_inverse.shape[1:], BF16),
        pltpu.VMEM((rows, nb), BF16),
        pltpu.VMEM((cols, nb), BF16),
        pltpu.VMEM((1, nb), F32),
        pltpu.VMEM((total_panels, panel), F32),
        pltpu.VMEM((n_z, per * panel, per_dev * panel), BF16),
        pltpu.VMEM((n_z, per * panel, per_dev * panel), BF16),
        pltpu.VMEM((n_z, 8, 128), jnp.int32),
        pltpu.SMEM((n_z, 8, 128), jnp.int32),
        pltpu.VMEM(tile_inverse.shape[1:], BF16),
        pltpu.VMEM((nb, rows), BF16),
        pltpu.VMEM((rows, nb), BF16),
        pltpu.VMEM((rows, rows), BF16),
        pltpu.VMEM((rows, rows), F32),
        pltpu.VMEM((cols, rows), F32),
        pltpu.VMEM((cols, nb), F32),
        pltpu.VMEM((cols, rows), F32),
        pltpu.VMEM((cols, rows), BF16),
        pltpu.VMEM((cols, 2 * per_dev * panel), F32),
        dma((tile_inverse.shape[1] + 4 + n_z,)), dma, dma((n_z,)), dma((n_z,)),
        dma((n_z,)), dma((n_z,)),
    ]
    for _, size in groups:
        scratch += [
            pltpu.VMEM((SOLVES, n_z, pb + 1, size, panel), BF16),
            pltpu.VMEM((SOLVES, n_sec, 2, per, size, panel), BF16),
            pltpu.VMEM((SOLVES, 2 * n_sec, per, size, panel), BF16),
            pltpu.VMEM((SOLVES, n_z, per, size, panel), BF16),
            pltpu.VMEM((SOLVES, 2, per_dev, size, panel), BF16),
            pltpu.VMEM((SOLVES, 2 * n_sec, per, size, panel), BF16),
            pltpu.VMEM((SOLVES + 1, total_panels, size, panel), BF16),
        ]
        for shape in ((n_z,), (2 * n_sec,), (n_z,), (2 * n_sec,), (n_z,), (n_z, n_sec), (n_z,)):
            scratch += [dma(shape), dma(shape)]
    leaf, link = pl.pallas_call(
        functools.partial(kernel, n_sec, n_dev, per, groups),
        out_shape=(
            jax.ShapeDtypeStruct((cols, nb), BF16),
            jax.ShapeDtypeStruct((cols, per_dev * panel), BF16),
        ),
        in_specs=[pl.BlockSpec(memory_space=pltpu.SMEM)]
        + [pl.BlockSpec(memory_space=pl.ANY)] * 6,
        out_specs=(vmem, vmem),
        scratch_shapes=scratch,
        compiler_params=pltpu.CompilerParams(
            collective_id=0, has_side_effects=True, vmem_limit_bytes=56 * 1024 * 1024
        ),
    )(
        link_panels, tile_inverse[0], link_coupling[0], leaf_rhs[0], leaf_scale,
        link_scale.reshape(total_panels, panel), link_inverse,
    )
    return leaf[None], link


def apply_tiles(tile_inv, vectors):
    columns = vectors.shape[0]
    blocked = vectors.reshape(columns, tile_inv.shape[0], tile_inv.shape[1])
    result = jnp.einsum("tab,ctb->cta", tile_inv, blocked, preferred_element_type=F32)
    return result.reshape(columns, -1)


def plain(tile_inverse, link_coupling, link_panels, leaf_rhs, leaf_scale, link_scale, link_inverse):
    tile_inv, coupling, leaf_gain = tile_inverse[0], link_coupling[0], leaf_scale[0]
    own_panels = link_panels[0]
    pb = own_panels.shape[0]
    panel = coupling.shape[0] // pb
    link_size = link_scale.shape[0]
    panel_count = link_size // panel
    matches = own_panels[:, None] == jnp.arange(panel_count, dtype=jnp.int32)[None, :]
    selector = matches.astype(BF16)
    spreader = matches.astype(F32)
    columns = leaf_rhs.shape[1]
    previous = jnp.zeros(leaf_rhs.shape[1:], BF16)
    linking = jnp.zeros((columns, link_size), BF16)
    for solve_index in range(SOLVES):
        corrected = leaf_rhs[0].astype(F32) - leaf_gain[None, :] * previous.astype(F32)
        corrected = corrected.astype(BF16)
        link_side = -link_scale[None, :] * linking.astype(F32)
        solved = apply_tiles(tile_inv, corrected).astype(BF16)
        touched = jnp.einsum("cn,rn->cr", solved, coupling, preferred_element_type=F32)
        touched = touched.reshape(columns, pb, panel)
        spread = jnp.einsum("csr,sq->cqr", touched, spreader).reshape(columns, link_size)
        section = lax.psum_scatter(
            spread.astype(BF16), "sec", scatter_dimension=1, tiled=True
        ).astype(F32)
        summed = lax.psum(section, "dev")
        width = summed.shape[1]
        own_slab = lax.dynamic_slice_in_dim(link_side, lax.axis_index("sec") * width, width, 1)
        link_rhs = (own_slab - summed).astype(BF16)
        partial_value = jnp.dot(link_rhs, link_inverse, preferred_element_type=F32)
        own_part = lax.psum(partial_value, "sec").astype(BF16)
        linking = lax.all_gather(own_part, "dev", axis=1, tiled=True)
        picked = jnp.einsum(
            "cqr,sq->csr", linking.reshape(columns, panel_count, panel), selector,
            preferred_element_type=F32,
        )
        picked = picked.reshape(columns, pb * panel).astype(BF16)
        pushed = jnp.dot(picked, coupling, preferred_element_type=F32)
        reduced = (corrected.astype(F32) - pushed).astype(BF16)
        previous = apply_tiles(tile_inv, reduced).astype(BF16)
    width = link_size // lax.axis_size("dev")
    link_out = lax.dynamic_slice_in_dim(linking, lax.axis_index("dev") * width, width, 1)
    return previous[None], link_out


def per_device(n_sec, n_dev, *args):
    link_coupling, link_panels, link_scale = args[1], args[2], args[5]
    panel = link_coupling.shape[1] // link_panels.shape[1]
    panels = link_scale.shape[0] // panel
    fits = n_dev % 2 == 0 and panels % (n_sec * n_dev) == 0 and panels <= 128
    if fits and n_sec > 1 and link_coupling.shape[0] == 1:
        return fused(n_sec, n_dev, panels // (n_sec * n_dev), *args)
    return plain(*args)


def solution(mesh):
    in_specs = (
        P(("sec", "dev"), None, None, None),
        P(("sec", "dev"), None, None),
        P(("sec", "dev"), None),
        P(("sec", "dev"), None, None),
        P(("sec", "dev"), None),
        P(),
        P("sec", "dev"),
    )
    out_specs = (P(("sec", "dev"), None, None), P(None, "dev"))
    body = functools.partial(per_device, mesh.shape["sec"], mesh.shape["dev"])
    return jax.shard_map(
        body, mesh=mesh, in_specs=in_specs, out_specs=out_specs, check_vma=False
    )
```

```python
import functools

import jax
import jax.numpy as jnp
from jax import lax
from jax.experimental import pallas as pl
from jax.experimental.pallas import tpu as pltpu
from jax.sharding import PartitionSpec as P

SOLVES = 5
F32 = jnp.float32
BF16 = jnp.bfloat16


def nn(a, b):
    return lax.dot_general(a, b, (((1,), (0,)), ((), ())), preferred_element_type=F32)


def nt(a, b):
    return lax.dot_general(a, b, (((1,), (1,)), ((), ())), preferred_element_type=F32)


PER_GROUP = 7
SEMS = 14


def kernel(n_sec, n_dev, per, groups, *refs):
    (panels_ref, tile_hbm, coup_hbm, rhs_hbm, scale_hbm, lscale_hbm, linv_hbm,
     leaf_out, link_out,
     tile_ref, coup_ref, rhs_ref, scale_ref, lscale_ref, wown, wother, slot_v, slot_s,
     tile_t, mmat, qmat, kmat, kacc, base, solved, umat, picked, part,
     in_sem, slot_sem, slot_send, slot_recv, w_send, w_recv) = refs[:34]
    rest = refs[34:]
    span = PER_GROUP + SEMS
    buffers = [rest[g * span:g * span + PER_GROUP] for g in range(len(groups))]
    sems = [rest[g * span + PER_GROUP:(g + 1) * span] for g in range(len(groups))]
    n_groups = range(len(groups))
    s = lax.axis_index("sec")
    d = lax.axis_index("dev")
    n_z = n_dev // 2
    z = d // 2
    c = d % 2
    partner = z * 2 + (1 - c)
    pb = panels_ref.shape[1]
    tiles, tile = tile_ref.shape[0], tile_ref.shape[1]
    panel = coup_ref.shape[0] // pb
    per_sec = n_dev * per
    per_dev = n_sec * per
    own_rhs = s * per_sec + d * per

    def remote(src, send, recv, target, dst=None):
        return pltpu.make_async_remote_copy(
            src_ref=src, dst_ref=src if dst is None else dst, send_sem=send, recv_sem=recv,
            device_id=target, device_id_type=pl.DeviceIdType.MESH,
        )

    def started(copies):
        for copy in copies:
            copy.start()
        return copies

    def on_z(j, core):
        return ((z - j + n_z) % n_z) * 2 + core

    def rows(g):
        return pl.ds(groups[g][0], groups[g][1])

    loads = []

    def load(src, dst):
        copy = pltpu.make_async_copy(src, dst, in_sem.at[len(loads)])
        copy.start()
        loads.append(copy)
        return copy

    rhs_load = load(rhs_hbm, rhs_ref)
    coup_load = load(coup_hbm, coup_ref)
    tile_loads = [load(tile_hbm.at[t], tile_ref.at[t]) for t in range(tiles)]
    scale_load = load(scale_hbm, scale_ref)
    lscale_load = load(lscale_hbm, lscale_ref)

    def inverse_rows(owner):
        depth = per * panel
        return linv_hbm.at[pl.ds(pl.multiple_of(owner * depth, depth), depth)]

    w_loads = [load(inverse_rows(i * 2 + c), wown.at[i]) for i in range(n_z)]

    barrier = pltpu.get_barrier_semaphore()
    def at_z(m):
        return {"sec": (s + m // 2) % n_sec, "dev": z * 2 + (c + m % 2) % 2}

    n_at_z = 2 * n_sec
    for j in range(1, n_z):
        pl.semaphore_signal(barrier, inc=1, device_id={"dev": on_z(j, c)},
                            device_id_type=pl.DeviceIdType.MESH)
    for m in range(1, n_at_z):
        pl.semaphore_signal(barrier, inc=1, device_id=at_z(m),
                            device_id_type=pl.DeviceIdType.MESH)

    for g in n_groups:
        tbuf, link = buffers[g][0], buffers[g][6]
        zero_panel = jnp.zeros(tbuf.shape[3:], BF16)
        for k in range(SOLVES):
            for i in range(n_z):
                tbuf[k, i, pb] = zero_panel
        for j in range(per):
            link[0, own_rhs + j] = zero_panel
    lane = lax.broadcasted_iota(jnp.int32, slot_v.shape[1:], 1)
    slots = jnp.full(slot_v.shape[1:], pb, jnp.int32)
    for q in range(pb):
        slots = jnp.where(lane == panels_ref[0, q], q, slots)
    slot_v[z] = slots

    rhs_load.wait()
    first = None
    for t in range(tiles):
        cols = pl.ds(t * tile, tile)
        tile_loads[t].wait()
        tile_t[t] = tile_ref[t].T
        value = nn(rhs_ref[:, cols], tile_t[t])
        solved[:, cols] = value
        if t == 0:
            coup_load.wait()
        term = nt(value.astype(BF16), coup_ref[:, cols])
        first = term if first is None else first + term
    base[...] = first

    pl.semaphore_wait(barrier, n_z - 1 + n_at_z - 1)

    def along_z(ref, send, recv):
        return [remote(ref, send.at[j], recv.at[j], {"dev": ((z + j) % n_z) * 2 + c})
                for j in range(1, n_z)]

    def to_core(ref, send, recv, j):
        return remote(ref, send.at[j], recv.at[j], {"dev": partner})

    def touched_sends(g, k):
        return along_z(buffers[g][0].at[k, z, pl.ds(0, pb)], sems[g][0], sems[g][1])

    def store_touched(g, k, value):
        for q in range(pb):
            buffers[g][0][k, z, q] = value[:, q * panel:(q + 1) * panel].astype(BF16)
        started(touched_sends(g, k))

    for g in n_groups:
        store_touched(g, 0, base[rows(g), :])
    slot_copies = started(along_z(slot_v.at[z], slot_send, slot_recv))
    w_copies = started([
        remote(inverse_rows(i * 2 + 1 - c), w_send.at[i], w_recv.at[i], {"dev": partner},
               wother.at[i])
        for i in range(n_z)
    ])
    scale_load.wait()
    lscale_load.wait()

    def solve(k, carry):
        sends = []
        t_sends = []

        @pl.when(k == 0)
        def _():
            for t in range(tiles):
                cols = pl.ds(t * tile, tile)
                mmat[cols, :] = nn(coup_ref[:, cols], tile_ref[t]).astype(BF16).T
                qmat[:, cols] = nn(coup_ref[:, cols], tile_t[t]).astype(BF16)
            for copy in slot_copies:
                copy.wait()
            to_smem = pltpu.make_async_copy(slot_v, slot_s, slot_sem)
            to_smem.start()
            to_smem.wait()

        @pl.when(k > 0)
        def _():
            for t in range(tiles):
                cols = pl.ds(t * tile, tile)
                leaf = solved[:, cols] - nn(picked[...], qmat[:, cols])
                x = rhs_ref[:, cols].astype(F32) - scale_ref[:, cols] * leaf
                solved[:, cols] = nn(x.astype(BF16), tile_t[t])

        r_copies = []
        for g in n_groups:
            tbuf, rsend, rrecv = buffers[g][0], buffers[g][1], buffers[g][2]
            copies = touched_sends(g, k)
            for copy in copies:
                copy.wait_recv()
            t_sends += copies
            for a in range(n_sec):
                for b in range(2):
                    for j in range(per):
                        q = a * per_sec + (z * 2 + b) * per + j
                        total = tbuf[k, 0, slot_s[0, 0, q]].astype(F32)
                        for i in range(1, n_z):
                            total = total + tbuf[k, i, slot_s[i, 0, q]].astype(F32)
                        rsend[k, a, b, j] = total.astype(BF16)
            r_copies.append(started([
                remote(rsend.at[k, (s + m // 2) % n_sec, (c + m % 2) % 2], sems[g][2].at[m],
                       sems[g][3].at[m], at_z(m), rrecv.at[k, m])
                for m in range(1, n_at_z)
            ]))
            sends += r_copies[g]

        h_copies = []
        for g in n_groups:
            _, rsend, rrecv, hbuf, _, _, link = buffers[g]
            totals = []
            for j in range(per):
                prev = link[k, own_rhs + j].astype(F32)
                totals.append(-lscale_ref[pl.ds(own_rhs + j, 1), :] * prev
                              - rsend[k, s, c, j].astype(F32))
            for copy in r_copies[g]:
                copy.wait_recv()
            for j in range(per):
                total = totals[j]
                for m in range(1, n_at_z):
                    total = total - rrecv[k, m, j].astype(F32)
                hbuf[k, z, j] = total.astype(BF16)
            h_copies.append(started(along_z(hbuf.at[k, z], sems[g][4], sems[g][5])))

        @pl.when(k == 0)
        def _():
            for copy in w_loads + w_copies:
                copy.wait()

        def multiply(g, owner):
            hbuf = buffers[g][3]
            left = jnp.concatenate([hbuf[k, owner, j] for j in range(per)], axis=1)
            return nn(left, wown[owner]), nn(left, wother[owner])

        half = per_dev * panel

        for g in n_groups:
            part[rows(g), :half], part[rows(g), half:] = multiply(g, z)

        @pl.when(k < SOLVES - 1)
        def _():
            total = base[...]
            for t in range(tiles):
                cols = pl.ds(t * tile, tile)
                scaled = (scale_ref[:, cols] * solved[:, cols]).astype(BF16)
                total = total - nn(scaled, mmat[cols, :])
            umat[...] = total

        l_copies = []
        for g in n_groups:
            hbuf, lsend, lrecv = buffers[g][3], buffers[g][4], buffers[g][5]
            copies = h_copies[g]
            for j in range(1, n_z):
                copies[j - 1].wait_recv()
                near, far = multiply(g, (z - j + n_z) % n_z)
                part[rows(g), :half] += near
                part[rows(g), half:] += far
            sends += copies
            for b in range(2):
                for q in range(per_dev):
                    at = b * half + q * panel
                    lsend[k, b, q] = part[rows(g), at:at + panel].astype(BF16)
            l_copies.append(started([
                remote(lsend.at[k, m % 2, pl.ds(((s + m // 2) % n_sec) * per, per)],
                       sems[g][6].at[m], sems[g][7].at[m], at_z(m), lrecv.at[k, m])
                for m in range(1, n_at_z)
            ]))
            sends += l_copies[g]

        @pl.when(k == 0)
        def _():
            for t in range(tiles):
                cols = pl.ds(t * tile, tile)
                scaled = (scale_ref[:, cols] * qmat[:, cols].astype(F32)).astype(BF16)
                term = nn(scaled, mmat[cols, :])
                if t == 0:
                    kacc[...] = term
                else:
                    kacc[...] += term
            kmat[...] = kacc[...].astype(BF16)

        def piece(g, owner, section):
            return buffers[g][6].at[k + 1, pl.ds(owner * per_dev + section * per, per)]

        z_copies = []
        for g in n_groups:
            lrecv, link = buffers[g][5], buffers[g][6]
            for copy in l_copies[g]:
                copy.wait_recv()
            for j in range(per):
                own_cols = pl.ds(pl.multiple_of((s * per + j) * panel, panel), panel)
                total = part[rows(g), own_cols]
                for m in range(1, n_at_z):
                    total = total + lrecv[k, m, j].astype(F32)
                link[k + 1, d * per_dev + s * per + j] = total.astype(BF16)
            z_copies.append(started(along_z(piece(g, d, s), sems[g][8], sems[g][9])))
            sends += z_copies[g]
        g_copies = []
        for g in n_groups:
            g_copies.append([])
            for i in range(n_z):
                if i > 0:
                    z_copies[g][i - 1].wait_recv()
                g_copies[g].append(started([
                    remote(piece(g, on_z(i, c), s), sems[g][10].at[i, j], sems[g][11].at[i, j],
                           {"sec": (s + j) % n_sec})
                    for j in range(1, n_sec)
                ]))
                sends += g_copies[g][i]
        c_copies = []
        for g in n_groups:
            c_copies.append([])
            for i in range(n_z):
                for copy in g_copies[g][i]:
                    copy.wait_recv()
                whole = buffers[g][6].at[k + 1, pl.ds(on_z(i, c) * per_dev, per_dev)]
                c_copies[g] += started([to_core(whole, sems[g][12], sems[g][13], i)])
            sends += c_copies[g]
        for copy in t_sends:
            copy.wait_send()
        for g in n_groups:
            for copy in c_copies[g]:
                copy.wait_recv()
            for q in range(pb):
                picked[rows(g), q * panel:(q + 1) * panel] = buffers[g][6][k + 1, panels_ref[0, q]]

            @pl.when(k < SOLVES - 1)
            def _():
                store_touched(g, k + 1, umat[rows(g), :] + nn(picked[rows(g), :], kmat[...]))

        for copy in sends:
            copy.wait_send()
        return carry

    lax.fori_loop(0, SOLVES, solve, 0)

    for t in range(tiles):
        cols = pl.ds(t * tile, tile)
        leaf_out[:, cols] = (solved[:, cols] - nn(picked[...], qmat[:, cols])).astype(BF16)
    for g in n_groups:
        for q in range(per_dev):
            link_out[rows(g), q * panel:(q + 1) * panel] = buffers[g][6][SOLVES, d * per_dev + q]


def fused(n_sec, n_dev, per, tile_inverse, link_coupling, link_panels, leaf_rhs, leaf_scale,
          link_scale, link_inverse):
    pb = link_panels.shape[1]
    rows, nb = link_coupling.shape[1:]
    panel = rows // pb
    cols = leaf_rhs.shape[1]
    total_panels = link_scale.shape[0] // panel
    per_dev = n_sec * per
    n_z = n_dev // 2
    groups = ((0, cols),)
    vmem = pl.BlockSpec(memory_space=pltpu.VMEM)
    dma = pltpu.SemaphoreType.DMA
    scratch = [
        pltpu.VMEM(tile_inverse.shape[1:], BF16),
        pltpu.VMEM((rows, nb), BF16),
        pltpu.VMEM((cols, nb), BF16),
        pltpu.VMEM((1, nb), F32),
        pltpu.VMEM((total_panels, panel), F32),
        pltpu.VMEM((n_z, per * panel, per_dev * panel), BF16),
        pltpu.VMEM((n_z, per * panel, per_dev * panel), BF16),
        pltpu.VMEM((n_z, 8, 128), jnp.int32),
        pltpu.SMEM((n_z, 8, 128), jnp.int32),
        pltpu.VMEM(tile_inverse.shape[1:], BF16),
        pltpu.VMEM((nb, rows), BF16),
        pltpu.VMEM((rows, nb), BF16),
        pltpu.VMEM((rows, rows), BF16),
        pltpu.VMEM((rows, rows), F32),
        pltpu.VMEM((cols, rows), F32),
        pltpu.VMEM((cols, nb), F32),
        pltpu.VMEM((cols, rows), F32),
        pltpu.VMEM((cols, rows), BF16),
        pltpu.VMEM((cols, 2 * per_dev * panel), F32),
        dma((tile_inverse.shape[1] + 4 + n_z,)), dma, dma((n_z,)), dma((n_z,)),
        dma((n_z,)), dma((n_z,)),
    ]
    for _, size in groups:
        scratch += [
            pltpu.VMEM((SOLVES, n_z, pb + 1, size, panel), BF16),
            pltpu.VMEM((SOLVES, n_sec, 2, per, size, panel), BF16),
            pltpu.VMEM((SOLVES, 2 * n_sec, per, size, panel), BF16),
            pltpu.VMEM((SOLVES, n_z, per, size, panel), BF16),
            pltpu.VMEM((SOLVES, 2, per_dev, size, panel), BF16),
            pltpu.VMEM((SOLVES, 2 * n_sec, per, size, panel), BF16),
            pltpu.VMEM((SOLVES + 1, total_panels, size, panel), BF16),
        ]
        for shape in ((n_z,), (2 * n_sec,), (n_z,), (2 * n_sec,), (n_z,), (n_z, n_sec), (n_z,)):
            scratch += [dma(shape), dma(shape)]
    leaf, link = pl.pallas_call(
        functools.partial(kernel, n_sec, n_dev, per, groups),
        out_shape=(
            jax.ShapeDtypeStruct((cols, nb), BF16),
            jax.ShapeDtypeStruct((cols, per_dev * panel), BF16),
        ),
        in_specs=[pl.BlockSpec(memory_space=pltpu.SMEM)]
        + [pl.BlockSpec(memory_space=pl.ANY)] * 6,
        out_specs=(vmem, vmem),
        scratch_shapes=scratch,
        compiler_params=pltpu.CompilerParams(
            collective_id=0, has_side_effects=True, vmem_limit_bytes=48 * 1024 * 1024
        ),
    )(
        link_panels, tile_inverse[0], link_coupling[0], leaf_rhs[0], leaf_scale,
        link_scale.reshape(total_panels, panel), link_inverse,
    )
    return leaf[None], link


def apply_tiles(tile_inv, vectors):
    columns = vectors.shape[0]
    blocked = vectors.reshape(columns, tile_inv.shape[0], tile_inv.shape[1])
    result = jnp.einsum("tab,ctb->cta", tile_inv, blocked, preferred_element_type=F32)
    return result.reshape(columns, -1)


def plain(tile_inverse, link_coupling, link_panels, leaf_rhs, leaf_scale, link_scale, link_inverse):
    tile_inv, coupling, leaf_gain = tile_inverse[0], link_coupling[0], leaf_scale[0]
    own_panels = link_panels[0]
    pb = own_panels.shape[0]
    panel = coupling.shape[0] // pb
    link_size = link_scale.shape[0]
    panel_count = link_size // panel
    matches = own_panels[:, None] == jnp.arange(panel_count, dtype=jnp.int32)[None, :]
    selector = matches.astype(BF16)
    spreader = matches.astype(F32)
    columns = leaf_rhs.shape[1]
    previous = jnp.zeros(leaf_rhs.shape[1:], BF16)
    linking = jnp.zeros((columns, link_size), BF16)
    for solve_index in range(SOLVES):
        corrected = leaf_rhs[0].astype(F32) - leaf_gain[None, :] * previous.astype(F32)
        corrected = corrected.astype(BF16)
        link_side = -link_scale[None, :] * linking.astype(F32)
        solved = apply_tiles(tile_inv, corrected).astype(BF16)
        touched = jnp.einsum("cn,rn->cr", solved, coupling, preferred_element_type=F32)
        touched = touched.reshape(columns, pb, panel)
        spread = jnp.einsum("csr,sq->cqr", touched, spreader).reshape(columns, link_size)
        section = lax.psum_scatter(
            spread.astype(BF16), "sec", scatter_dimension=1, tiled=True
        ).astype(F32)
        summed = lax.psum(section, "dev")
        width = summed.shape[1]
        own_slab = lax.dynamic_slice_in_dim(link_side, lax.axis_index("sec") * width, width, 1)
        link_rhs = (own_slab - summed).astype(BF16)
        partial_value = jnp.dot(link_rhs, link_inverse, preferred_element_type=F32)
        own_part = lax.psum(partial_value, "sec").astype(BF16)
        linking = lax.all_gather(own_part, "dev", axis=1, tiled=True)
        picked = jnp.einsum(
            "cqr,sq->csr", linking.reshape(columns, panel_count, panel), selector,
            preferred_element_type=F32,
        )
        picked = picked.reshape(columns, pb * panel).astype(BF16)
        pushed = jnp.dot(picked, coupling, preferred_element_type=F32)
        reduced = (corrected.astype(F32) - pushed).astype(BF16)
        previous = apply_tiles(tile_inv, reduced).astype(BF16)
    width = link_size // lax.axis_size("dev")
    link_out = lax.dynamic_slice_in_dim(linking, lax.axis_index("dev") * width, width, 1)
    return previous[None], link_out


def per_device(n_sec, n_dev, *args):
    link_coupling, link_panels, link_scale = args[1], args[2], args[5]
    panel = link_coupling.shape[1] // link_panels.shape[1]
    panels = link_scale.shape[0] // panel
    fits = n_dev % 2 == 0 and panels % (n_sec * n_dev) == 0 and panels <= 128
    if fits and n_sec > 1 and link_coupling.shape[0] == 1:
        return fused(n_sec, n_dev, panels // (n_sec * n_dev), *args)
    return plain(*args)


def solution(mesh):
    in_specs = (
        P(("sec", "dev"), None, None, None),
        P(("sec", "dev"), None, None),
        P(("sec", "dev"), None),
        P(("sec", "dev"), None, None),
        P(("sec", "dev"), None),
        P(),
        P("sec", "dev"),
    )
    out_specs = (P(("sec", "dev"), None, None), P(None, "dev"))
    body = functools.partial(per_device, mesh.shape["sec"], mesh.shape["dev"])
    return jax.shard_map(
        body, mesh=mesh, in_specs=in_specs, out_specs=out_specs, check_vma=False
    )
```

```python
import functools

import jax
import jax.numpy as jnp
from jax import lax
from jax.experimental import pallas as pl
from jax.experimental.pallas import tpu as pltpu
from jax.sharding import PartitionSpec as P

SOLVES = 5
F32 = jnp.float32
BF16 = jnp.bfloat16


def nn(a, b):
    return lax.dot_general(a, b, (((1,), (0,)), ((), ())), preferred_element_type=F32)


def nt(a, b):
    return lax.dot_general(a, b, (((1,), (1,)), ((), ())), preferred_element_type=F32)


PER_GROUP = 7
SEMS = 14


def kernel(n_sec, n_dev, per, groups, *refs):
    (panels_ref, tile_hbm, coup_hbm, rhs_hbm, scale_hbm, lscale_hbm, linv_hbm,
     leaf_out, link_out,
     tile_ref, coup_ref, rhs_ref, scale_ref, lscale_ref, wown, wother, slot_v, slot_s,
     tile_t, mmat, qmat, kmat, kacc, base, solved, umat, picked, part,
     in_sem, slot_sem, slot_send, slot_recv, w_send, w_recv) = refs[:34]
    rest = refs[34:]
    span = PER_GROUP + SEMS
    buffers = [rest[g * span:g * span + PER_GROUP] for g in range(len(groups))]
    sems = [rest[g * span + PER_GROUP:(g + 1) * span] for g in range(len(groups))]
    n_groups = range(len(groups))
    s = lax.axis_index("sec")
    d = lax.axis_index("dev")
    n_z = n_dev // 2
    z = d // 2
    c = d % 2
    partner = z * 2 + (1 - c)
    pb = panels_ref.shape[1]
    tiles, tile = tile_ref.shape[0], tile_ref.shape[1]
    panel = coup_ref.shape[0] // pb
    per_sec = n_dev * per
    per_dev = n_sec * per
    own_rhs = s * per_sec + d * per

    def remote(src, send, recv, target, dst=None):
        return pltpu.make_async_remote_copy(
            src_ref=src, dst_ref=src if dst is None else dst, send_sem=send, recv_sem=recv,
            device_id=target, device_id_type=pl.DeviceIdType.MESH,
        )

    def started(copies):
        for copy in copies:
            copy.start()
        return copies

    def on_z(j, core):
        return ((z - j + n_z) % n_z) * 2 + core

    def rows(g):
        return pl.ds(groups[g][0], groups[g][1])

    loads = []

    def load(src, dst):
        copy = pltpu.make_async_copy(src, dst, in_sem.at[len(loads)])
        copy.start()
        loads.append(copy)
        return copy

    rhs_load = load(rhs_hbm, rhs_ref)
    coup_load = load(coup_hbm, coup_ref)
    tile_loads = [load(tile_hbm.at[t], tile_ref.at[t]) for t in range(tiles)]
    scale_load = load(scale_hbm, scale_ref)
    lscale_load = load(lscale_hbm, lscale_ref)

    def inverse_rows(owner):
        depth = per * panel
        return linv_hbm.at[pl.ds(pl.multiple_of(owner * depth, depth), depth)]

    w_loads = [load(inverse_rows(i * 2 + c), wown.at[i]) for i in range(n_z)]

    barrier = pltpu.get_barrier_semaphore()
    def at_z(m):
        return {"sec": (s + m // 2) % n_sec, "dev": z * 2 + (c + m % 2) % 2}

    n_at_z = 2 * n_sec
    for j in range(1, n_z):
        pl.semaphore_signal(barrier, inc=1, device_id={"dev": on_z(j, c)},
                            device_id_type=pl.DeviceIdType.MESH)
    for m in range(1, n_at_z):
        pl.semaphore_signal(barrier, inc=1, device_id=at_z(m),
                            device_id_type=pl.DeviceIdType.MESH)

    for g in n_groups:
        tbuf, link = buffers[g][0], buffers[g][6]
        zero_panel = jnp.zeros(tbuf.shape[3:], BF16)
        for k in range(SOLVES):
            for i in range(n_z):
                tbuf[k, i, pb] = zero_panel
        for j in range(per):
            link[0, own_rhs + j] = zero_panel
    lane = lax.broadcasted_iota(jnp.int32, slot_v.shape[1:], 1)
    slots = jnp.full(slot_v.shape[1:], pb, jnp.int32)
    for q in range(pb):
        slots = jnp.where(lane == panels_ref[0, q], q, slots)
    slot_v[z] = slots

    rhs_load.wait()
    first = None
    for t in range(tiles):
        cols = pl.ds(t * tile, tile)
        tile_loads[t].wait()
        tile_t[t] = tile_ref[t].T
        value = nn(rhs_ref[:, cols], tile_t[t])
        solved[:, cols] = value
        if t == 0:
            coup_load.wait()
        term = nt(value.astype(BF16), coup_ref[:, cols])
        first = term if first is None else first + term
    base[...] = first

    pl.semaphore_wait(barrier, n_z - 1 + n_at_z - 1)

    def along_z(ref, send, recv):
        return [remote(ref, send.at[j], recv.at[j], {"dev": ((z + j) % n_z) * 2 + c})
                for j in range(1, n_z)]

    def to_core(ref, send, recv, j):
        return remote(ref, send.at[j], recv.at[j], {"dev": partner})

    def touched_sends(g, k):
        return along_z(buffers[g][0].at[k, z, pl.ds(0, pb)], sems[g][0], sems[g][1])

    def store_touched(g, k, value):
        for q in range(pb):
            buffers[g][0][k, z, q] = value[:, q * panel:(q + 1) * panel].astype(BF16)
        started(touched_sends(g, k))

    for g in n_groups:
        store_touched(g, 0, base[rows(g), :])
    slot_copies = started(along_z(slot_v.at[z], slot_send, slot_recv))
    w_copies = started([
        remote(inverse_rows(i * 2 + 1 - c), w_send.at[i], w_recv.at[i], {"dev": partner},
               wother.at[i])
        for i in range(n_z)
    ])
    scale_load.wait()
    lscale_load.wait()

    def solve(k, carry):
        sends = []
        t_sends = []

        @pl.when(k == 0)
        def _():
            for t in range(tiles):
                cols = pl.ds(t * tile, tile)
                mmat[cols, :] = nn(coup_ref[:, cols], tile_ref[t]).astype(BF16).T
                qmat[:, cols] = nn(coup_ref[:, cols], tile_t[t]).astype(BF16)
            for copy in slot_copies:
                copy.wait()
            to_smem = pltpu.make_async_copy(slot_v, slot_s, slot_sem)
            to_smem.start()
            to_smem.wait()

        @pl.when(k > 0)
        def _():
            for t in range(tiles):
                cols = pl.ds(t * tile, tile)
                leaf = solved[:, cols] - nn(picked[...], qmat[:, cols])
                x = rhs_ref[:, cols].astype(F32) - scale_ref[:, cols] * leaf
                solved[:, cols] = nn(x.astype(BF16), tile_t[t])

        r_copies = []
        for g in n_groups:
            tbuf, rsend, rrecv = buffers[g][0], buffers[g][1], buffers[g][2]
            copies = touched_sends(g, k)
            for copy in copies:
                copy.wait_recv()
            t_sends += copies
            for a in range(n_sec):
                for b in range(2):
                    for j in range(per):
                        q = a * per_sec + (z * 2 + b) * per + j
                        total = tbuf[k, 0, slot_s[0, 0, q]].astype(F32)
                        for i in range(1, n_z):
                            total = total + tbuf[k, i, slot_s[i, 0, q]].astype(F32)
                        rsend[k, a, b, j] = total.astype(BF16)
            r_copies.append(started([
                remote(rsend.at[k, (s + m // 2) % n_sec, (c + m % 2) % 2], sems[g][2].at[m],
                       sems[g][3].at[m], at_z(m), rrecv.at[k, m])
                for m in range(1, n_at_z)
            ]))
            sends += r_copies[g]

        h_copies = []
        for g in n_groups:
            _, rsend, rrecv, hbuf, _, _, link = buffers[g]
            totals = []
            for j in range(per):
                prev = link[k, own_rhs + j].astype(F32)
                totals.append(-lscale_ref[pl.ds(own_rhs + j, 1), :] * prev
                              - rsend[k, s, c, j].astype(F32))
            for copy in r_copies[g]:
                copy.wait_recv()
            for j in range(per):
                total = totals[j]
                for m in range(1, n_at_z):
                    total = total - rrecv[k, m, j].astype(F32)
                hbuf[k, z, j] = total.astype(BF16)
            h_copies.append(started(along_z(hbuf.at[k, z], sems[g][4], sems[g][5])))

        @pl.when(k == 0)
        def _():
            for copy in w_loads + w_copies:
                copy.wait()

        def multiply(g, owner):
            hbuf = buffers[g][3]
            left = jnp.concatenate([hbuf[k, owner, j] for j in range(per)], axis=1)
            return nn(left, wown[owner]), nn(left, wother[owner])

        half = per_dev * panel

        for g in n_groups:
            part[rows(g), :half], part[rows(g), half:] = multiply(g, z)

        @pl.when(k < SOLVES - 1)
        def _():
            total = base[...]
            for t in range(tiles):
                cols = pl.ds(t * tile, tile)
                scaled = (scale_ref[:, cols] * solved[:, cols]).astype(BF16)
                total = total - nn(scaled, mmat[cols, :])
            umat[...] = total

        l_copies = []
        for g in n_groups:
            hbuf, lsend, lrecv = buffers[g][3], buffers[g][4], buffers[g][5]
            copies = h_copies[g]
            for j in range(1, n_z):
                copies[j - 1].wait_recv()
                near, far = multiply(g, (z - j + n_z) % n_z)
                part[rows(g), :half] += near
                part[rows(g), half:] += far
            sends += copies
            for b in range(2):
                for q in range(per_dev):
                    at = b * half + q * panel
                    lsend[k, b, q] = part[rows(g), at:at + panel].astype(BF16)
            l_copies.append(started([
                remote(lsend.at[k, m % 2, pl.ds(((s + m // 2) % n_sec) * per, per)],
                       sems[g][6].at[m], sems[g][7].at[m], at_z(m), lrecv.at[k, m])
                for m in range(1, n_at_z)
            ]))
            sends += l_copies[g]

        @pl.when(k == 0)
        def _():
            for t in range(tiles):
                cols = pl.ds(t * tile, tile)
                scaled = (scale_ref[:, cols] * qmat[:, cols].astype(F32)).astype(BF16)
                term = nn(scaled, mmat[cols, :])
                if t == 0:
                    kacc[...] = term
                else:
                    kacc[...] += term
            kmat[...] = kacc[...].astype(BF16)

        def piece(g, owner, section):
            return buffers[g][6].at[k + 1, pl.ds(owner * per_dev + section * per, per)]

        z_copies = []
        for g in n_groups:
            lrecv, link = buffers[g][5], buffers[g][6]
            for copy in l_copies[g]:
                copy.wait_recv()
            for j in range(per):
                own_cols = pl.ds(pl.multiple_of((s * per + j) * panel, panel), panel)
                total = part[rows(g), own_cols]
                for m in range(1, n_at_z):
                    total = total + lrecv[k, m, j].astype(F32)
                link[k + 1, d * per_dev + s * per + j] = total.astype(BF16)
            z_copies.append(started(along_z(piece(g, d, s), sems[g][8], sems[g][9])))
            sends += z_copies[g]
        g_copies = []
        for g in n_groups:
            g_copies.append([])
            for i in range(n_z):
                if i > 0:
                    z_copies[g][i - 1].wait_recv()
                g_copies[g].append(started([
                    remote(piece(g, on_z(i, c), s), sems[g][10].at[i, j], sems[g][11].at[i, j],
                           {"sec": (s + j) % n_sec})
                    for j in range(1, n_sec)
                ]))
                sends += g_copies[g][i]
        c_copies = []
        for g in n_groups:
            c_copies.append([])
            for i in range(n_z):
                for copy in g_copies[g][i]:
                    copy.wait_recv()
                whole = buffers[g][6].at[k + 1, pl.ds(on_z(i, c) * per_dev, per_dev)]
                c_copies[g] += started([to_core(whole, sems[g][12], sems[g][13], i)])
            sends += c_copies[g]
        for copy in t_sends:
            copy.wait_send()
        for g in n_groups:
            for copy in c_copies[g]:
                copy.wait_recv()
            for q in range(pb):
                picked[rows(g), q * panel:(q + 1) * panel] = buffers[g][6][k + 1, panels_ref[0, q]]

            @pl.when(k < SOLVES - 1)
            def _():
                store_touched(g, k + 1, umat[rows(g), :] + nn(picked[rows(g), :], kmat[...]))

        for copy in sends:
            copy.wait_send()
        return carry

    lax.fori_loop(0, SOLVES, solve, 0)

    for t in range(tiles):
        cols = pl.ds(t * tile, tile)
        leaf_out[:, cols] = (solved[:, cols] - nn(picked[...], qmat[:, cols])).astype(BF16)
    for g in n_groups:
        for q in range(per_dev):
            link_out[rows(g), q * panel:(q + 1) * panel] = buffers[g][6][SOLVES, d * per_dev + q]


def row_groups(cols):
    size = 16 if cols % 16 == 0 else cols
    return tuple((start, size) for start in range(0, cols, size))


def fused(n_sec, n_dev, per, tile_inverse, link_coupling, link_panels, leaf_rhs, leaf_scale,
          link_scale, link_inverse):
    pb = link_panels.shape[1]
    rows, nb = link_coupling.shape[1:]
    panel = rows // pb
    cols = leaf_rhs.shape[1]
    total_panels = link_scale.shape[0] // panel
    per_dev = n_sec * per
    n_z = n_dev // 2
    groups = row_groups(cols)
    vmem = pl.BlockSpec(memory_space=pltpu.VMEM)
    dma = pltpu.SemaphoreType.DMA
    scratch = [
        pltpu.VMEM(tile_inverse.shape[1:], BF16),
        pltpu.VMEM((rows, nb), BF16),
        pltpu.VMEM((cols, nb), BF16),
        pltpu.VMEM((1, nb), F32),
        pltpu.VMEM((total_panels, panel), F32),
        pltpu.VMEM((n_z, per * panel, per_dev * panel), BF16),
        pltpu.VMEM((n_z, per * panel, per_dev * panel), BF16),
        pltpu.VMEM((n_z, 8, 128), jnp.int32),
        pltpu.SMEM((n_z, 8, 128), jnp.int32),
        pltpu.VMEM(tile_inverse.shape[1:], BF16),
        pltpu.VMEM((nb, rows), BF16),
        pltpu.VMEM((rows, nb), BF16),
        pltpu.VMEM((rows, rows), BF16),
        pltpu.VMEM((rows, rows), F32),
        pltpu.VMEM((cols, rows), F32),
        pltpu.VMEM((cols, nb), F32),
        pltpu.VMEM((cols, rows), F32),
        pltpu.VMEM((cols, rows), BF16),
        pltpu.VMEM((cols, 2 * per_dev * panel), F32),
        dma((tile_inverse.shape[1] + 4 + n_z,)), dma, dma((n_z,)), dma((n_z,)),
        dma((n_z,)), dma((n_z,)),
    ]
    for _, size in groups:
        scratch += [
            pltpu.VMEM((SOLVES, n_z, pb + 1, size, panel), BF16),
            pltpu.VMEM((SOLVES, n_sec, 2, per, size, panel), BF16),
            pltpu.VMEM((SOLVES, 2 * n_sec, per, size, panel), BF16),
            pltpu.VMEM((SOLVES, n_z, per, size, panel), BF16),
            pltpu.VMEM((SOLVES, 2, per_dev, size, panel), BF16),
            pltpu.VMEM((SOLVES, 2 * n_sec, per, size, panel), BF16),
            pltpu.VMEM((SOLVES + 1, total_panels, size, panel), BF16),
        ]
        for shape in ((n_z,), (2 * n_sec,), (n_z,), (2 * n_sec,), (n_z,), (n_z, n_sec), (n_z,)):
            scratch += [dma(shape), dma(shape)]
    leaf, link = pl.pallas_call(
        functools.partial(kernel, n_sec, n_dev, per, groups),
        out_shape=(
            jax.ShapeDtypeStruct((cols, nb), BF16),
            jax.ShapeDtypeStruct((cols, per_dev * panel), BF16),
        ),
        in_specs=[pl.BlockSpec(memory_space=pltpu.SMEM)]
        + [pl.BlockSpec(memory_space=pl.ANY)] * 6,
        out_specs=(vmem, vmem),
        scratch_shapes=scratch,
        compiler_params=pltpu.CompilerParams(
            collective_id=0, has_side_effects=True, vmem_limit_bytes=56 * 1024 * 1024
        ),
    )(
        link_panels, tile_inverse[0], link_coupling[0], leaf_rhs[0], leaf_scale,
        link_scale.reshape(total_panels, panel), link_inverse,
    )
    return leaf[None], link


def apply_tiles(tile_inv, vectors):
    columns = vectors.shape[0]
    blocked = vectors.reshape(columns, tile_inv.shape[0], tile_inv.shape[1])
    result = jnp.einsum("tab,ctb->cta", tile_inv, blocked, preferred_element_type=F32)
    return result.reshape(columns, -1)


def plain(tile_inverse, link_coupling, link_panels, leaf_rhs, leaf_scale, link_scale, link_inverse):
    tile_inv, coupling, leaf_gain = tile_inverse[0], link_coupling[0], leaf_scale[0]
    own_panels = link_panels[0]
    pb = own_panels.shape[0]
    panel = coupling.shape[0] // pb
    link_size = link_scale.shape[0]
    panel_count = link_size // panel
    matches = own_panels[:, None] == jnp.arange(panel_count, dtype=jnp.int32)[None, :]
    selector = matches.astype(BF16)
    spreader = matches.astype(F32)
    columns = leaf_rhs.shape[1]
    previous = jnp.zeros(leaf_rhs.shape[1:], BF16)
    linking = jnp.zeros((columns, link_size), BF16)
    for solve_index in range(SOLVES):
        corrected = leaf_rhs[0].astype(F32) - leaf_gain[None, :] * previous.astype(F32)
        corrected = corrected.astype(BF16)
        link_side = -link_scale[None, :] * linking.astype(F32)
        solved = apply_tiles(tile_inv, corrected).astype(BF16)
        touched = jnp.einsum("cn,rn->cr", solved, coupling, preferred_element_type=F32)
        touched = touched.reshape(columns, pb, panel)
        spread = jnp.einsum("csr,sq->cqr", touched, spreader).reshape(columns, link_size)
        section = lax.psum_scatter(
            spread.astype(BF16), "sec", scatter_dimension=1, tiled=True
        ).astype(F32)
        summed = lax.psum(section, "dev")
        width = summed.shape[1]
        own_slab = lax.dynamic_slice_in_dim(link_side, lax.axis_index("sec") * width, width, 1)
        link_rhs = (own_slab - summed).astype(BF16)
        partial_value = jnp.dot(link_rhs, link_inverse, preferred_element_type=F32)
        own_part = lax.psum(partial_value, "sec").astype(BF16)
        linking = lax.all_gather(own_part, "dev", axis=1, tiled=True)
        picked = jnp.einsum(
            "cqr,sq->csr", linking.reshape(columns, panel_count, panel), selector,
            preferred_element_type=F32,
        )
        picked = picked.reshape(columns, pb * panel).astype(BF16)
        pushed = jnp.dot(picked, coupling, preferred_element_type=F32)
        reduced = (corrected.astype(F32) - pushed).astype(BF16)
        previous = apply_tiles(tile_inv, reduced).astype(BF16)
    width = link_size // lax.axis_size("dev")
    link_out = lax.dynamic_slice_in_dim(linking, lax.axis_index("dev") * width, width, 1)
    return previous[None], link_out


def per_device(n_sec, n_dev, *args):
    link_coupling, link_panels, link_scale = args[1], args[2], args[5]
    panel = link_coupling.shape[1] // link_panels.shape[1]
    panels = link_scale.shape[0] // panel
    fits = n_dev % 2 == 0 and panels % (n_sec * n_dev) == 0 and panels <= 128
    if fits and n_sec > 1 and link_coupling.shape[0] == 1:
        return fused(n_sec, n_dev, panels // (n_sec * n_dev), *args)
    return plain(*args)


def solution(mesh):
    in_specs = (
        P(("sec", "dev"), None, None, None),
        P(("sec", "dev"), None, None),
        P(("sec", "dev"), None),
        P(("sec", "dev"), None, None),
        P(("sec", "dev"), None),
        P(),
        P("sec", "dev"),
    )
    out_specs = (P(("sec", "dev"), None, None), P(None, "dev"))
    body = functools.partial(per_device, mesh.shape["sec"], mesh.shape["dev"])
    return jax.shard_map(
        body, mesh=mesh, in_specs=in_specs, out_specs=out_specs, check_vma=False
    )
```
